128 devices in a mesh: gx: 16 (over x_lo, z, core), gy: 8 (over x_hi, y).
Axes of the slice: x: 4 (x_hi: 2, x_lo: 2; x = x_hi * 2 + x_lo), y: 4, z: 4, core: 2. Of those that a mesh axis runs over, the one named last changes fastest.
Arguments:
- level_set: float32 [1024, 320, 128], P('gx', 'gy'), may hold values from -6 to 6
- band_mask: int32 [1024, 320], P('gx', 'gy'), may hold values 0 or 1
- rows: float32 [131072, 128], P(('gx', 'gy')), may hold values from -1.5 to 1.5
- row_owner: int32 [131072, 1], P(('gx', 'gy')), may hold values from 0 to 127; in each aligned block of 1024 rows (0 to 1023, 1024 to 2047, ...) at most 16 rows name the same one
- row_tile: int32 [131072], P(('gx', 'gy')), may hold values from 0 to 2559, as said below
Outputs:
- updated: float32 [1024, 320, 128], P('gx', 'gy')
The draws below stay inside these ranges and needn't reach their ends.
Inputs may be any that keep to these rules, and one draw needn't show every extreme that they name: `row_owner`: owner of each row, devices numbered with gy fastest; among the rows of one device no owner is named more than 16 times, a bound that some block reaches. `row_tile`: column a * 40 + b of the owner's block is the cell column at local position (a, b).
All inputs are finite; a program needn't handle non-finite values. No bound on the sum of `band_mask` on one device may be relied on, other than what follows from the above.
Results may differ from the reference program's by a relative error of at most 0.0003.
Values sent between devices are 32-bit elements; how exact they have to be, the bound alone decides.
No kernel may reach another device: no remote copies, remote signals or barrier semaphores. Data moves between devices by JAX's collectives and lax.ppermute only.
A program may use at most 128 MiB of HBM per device.

```python
import math
import jax
import jax.numpy as jnp
import numpy as np

CX = 64
CY = 40
NZ = 128
ROWS_DEV = 1024
STEPS = 3
SWEEPS = 2
NX = 1024
NY = 320
ROWS_ALL = 131072
CAP = 16
N_GY = 8
DEVICES = 128


def draw_row_tile(key, part):
    keys = jax.random.split(jax.random.fold_in(key, 7), 4)
    count = ROWS_ALL
    across = jax.random.randint(keys[0], (count,), 0, CX, dtype=jnp.int32)
    along = jax.random.randint(keys[1], (count,), 0, CY, dtype=jnp.int32)
    kind = jax.random.randint(keys[2], (count,), 0, 4, dtype=jnp.int32)
    depth = jax.random.randint(keys[3], (count,), 0, 6, dtype=jnp.int32)
    edge_across = jnp.where(depth < 3, depth, CX - 6 + depth)
    edge_along = jnp.where(depth < 3, depth, CY - 6 + depth)
    across = jnp.where(kind == 1, edge_across, across)
    along = jnp.where(kind >= 2, edge_along, along)
    tile = (across * CY + along).astype(jnp.int32)
    tile = tile.at[0].set(0)
    tile = tile.at[count - 1].set(CX * CY - 1)
    return tile


def plant(result, rng, smallest, largest):
    extent = result.shape
    place = [jax.random.randint(jax.random.fold_in(rng, axis), (), 0, extent[axis]) for axis in range(len(extent))]
    result = result.at[tuple(place)].set(smallest)
    longest = extent.index(max(extent))
    place[longest] = (place[longest] + 1) % extent[longest]
    return result.at[tuple(place)].set(largest)


def level_of(rng, dims, pieces, least, top_value):
    factor_of, own = 1.0, jax.random.fold_in(rng, 6)
    for axis_at, blocks in pieces:
        steps = jnp.exp(jax.random.uniform(jax.random.fold_in(own, axis_at), (blocks,), jnp.float32, least / len(pieces), top_value / len(pieces)))
        factor_of = factor_of * jnp.repeat(steps, dims[axis_at] // blocks).reshape([-1 if axis == axis_at else 1 for axis in range(len(dims))])
    return factor_of


def routed_block(key, own, number, rows, count, top, bound, lean):
    order = jax.random.permutation(key, count)
    heavy_load, usual = load_shares(count, rows * top, bound, lean, True), load_shares(count, rows * top, bound, lean, False)
    places = jnp.arange(count)

    def named(sizes, turn):
        used = int((sizes > 0).sum())
        fixed = max(1, used // 4)
        moved = fixed + (places - fixed + turn * (used - fixed)) % max(1, count - fixed)
        return jnp.zeros((count,), jnp.int32).at[order[jnp.where(places < fixed, places, moved)]].set(jnp.asarray(sizes, jnp.int32))

    sizes = jnp.where(number % 4 == 0, named(heavy_load, number // 4), named(usual, number - number // 4 - 1))
    mixed = jax.random.permutation(jax.random.fold_in(own, 3), count)
    source_of, sink = mixed[0:count // 2 * 2:2], mixed[1:count // 2 * 2:2]
    slack = jnp.minimum(sizes[source_of] - 1, bound - sizes[sink]) // 2
    slack = jnp.where((source_of == order[0]) | (sink == order[0]) | (sizes[sink] == 0), 0, jnp.maximum(slack, 0))
    moved = jax.random.randint(jax.random.fold_in(own, 4), (count // 2,), 0, 1 << 20) % (slack + 1)
    sizes = sizes.at[source_of].add(-moved).at[sink].add(moved)
    members = jnp.searchsorted(jnp.cumsum(sizes), jnp.arange(rows * top), side="right").astype(jnp.int32)
    grid = members.reshape(top, rows).T
    grid = grid[jax.random.permutation(jax.random.fold_in(own, 1), rows)]
    turn = jax.random.randint(jax.random.fold_in(own, 2), (rows, 1), 0, top)
    return jnp.take_along_axis(grid, (jnp.arange(top)[None, :] + turn) % top, axis=1)


def load_shares(amount, total, most, slope, full):
    weights = [(1 << 20) // math.isqrt(rank ** slope) + 1 for rank in range(1, amount + 1)]
    largest = most if full else min(most, max(-(-total // amount), total * weights[0] // sum(weights)))
    least = 1 if total - largest >= amount - 1 else 0
    given, rest = [largest] + [least] * (amount - 1), total - largest - least * (amount - 1)
    while rest > 0:
        free = [i for i in range(1, amount) if given[i] < largest] or [i for i in range(1, amount) if given[i] < most]
        pool, left = sum([weights[i] for i in free]), rest
        for i in free:
            addition = min(most - given[i], max(1, left * weights[i] // pool), rest)
            given[i] = given[i] + addition
            rest = rest - addition
    return np.array(given)


def centred(key, extent, scale, bound, cuts=(), kind=jnp.bfloat16):
    drawn = scale * jax.random.normal(key, extent, jnp.float32)
    if cuts:
        drawn = drawn * level_of(key, extent, cuts, -0.22, 0.18)
    return jnp.clip(drawn, -bound, bound).astype(kind)


def setup_inputs(seed: int = 0) -> dict:
    seeds = jax.random.split(jax.random.key(seed), 6)
    level_set = centred(seeds[0], (NX, NY, NZ), 1.0, 6.0, ((0, 16), (1, 8)), jnp.float32)
    band_mask = plant((jax.random.randint(seeds[1], (NX, NY), 0, 16) < 15).astype(jnp.int32), jax.random.fold_in(seeds[1], 1), 0, 1)
    rows = jnp.clip(jax.random.uniform(seeds[2], (ROWS_ALL, NZ), jnp.float32, -1.5, 1.5) * level_of(seeds[2], (ROWS_ALL, NZ), ((0, 128),), -0.4, 0.0), -1.5, 1.5)
    row_owner_keys = jax.random.split(jax.random.fold_in(seeds[3], 1), ROWS_ALL // ROWS_DEV)
    row_owner_turns = jax.random.permutation(jax.random.fold_in(seeds[3], 3), ROWS_ALL // ROWS_DEV)
    row_owner = jax.vmap(lambda own, number: routed_block(jax.random.fold_in(seeds[3], 2), own, number, ROWS_DEV, DEVICES, 1, CAP, 2))(row_owner_keys, row_owner_turns).reshape((ROWS_ALL, 1))
    row_tile = draw_row_tile(jax.random.fold_in(seeds[5], 71), 0)
    return {"level_set": level_set, "band_mask": band_mask, "rows": rows, "row_owner": row_owner, "row_tile": row_tile}


EPSILON = 1e-06
TIME_STEP = 0.2
PSEUDO_STEP = 0.3

def weno_value(first, second, third, fourth, fifth):
    cand_one = first / 3.0 - 7.0 * second / 6.0 + 11.0 * third / 6.0
    cand_two = -second / 6.0 + 5.0 * third / 6.0 + fourth / 3.0
    cand_three = third / 3.0 + 5.0 * fourth / 6.0 - fifth / 6.0
    smooth_one = 13.0 / 12.0 * (first - 2.0 * second + third) ** 2 + 0.25 * (first - 4.0 * second + 3.0 * third) ** 2
    smooth_two = 13.0 / 12.0 * (second - 2.0 * third + fourth) ** 2 + 0.25 * (second - fourth) ** 2
    smooth_three = 13.0 / 12.0 * (third - 2.0 * fourth + fifth) ** 2 + 0.25 * (3.0 * third - 4.0 * fourth + fifth) ** 2
    weight_one = 0.1 / (EPSILON + smooth_one) ** 2
    weight_two = 0.6 / (EPSILON + smooth_two) ** 2
    weight_three = 0.3 / (EPSILON + smooth_three) ** 2
    total = weight_one + weight_two + weight_three
    return (weight_one * cand_one + weight_two * cand_two + weight_three * cand_three) / total

def hj_rate(shifted, speed):
    upper = 0.0
    lower = 0.0
    for axis in range(3):
        diffs = [shifted(axis, offset + 1) - shifted(axis, offset) for offset in range(-3, 3)]
        minus = weno_value(diffs[0], diffs[1], diffs[2], diffs[3], diffs[4])
        plus = weno_value(diffs[5], diffs[4], diffs[3], diffs[2], diffs[1])
        upper = upper + jnp.maximum(jnp.maximum(minus, 0.0) ** 2, jnp.minimum(plus, 0.0) ** 2)
        lower = lower + jnp.maximum(jnp.minimum(minus, 0.0) ** 2, jnp.maximum(plus, 0.0) ** 2)
    return -speed * jnp.sqrt(jnp.where(speed >= 0.0, upper, lower))

def reinit_rate(shifted, centre, sign):
    upper = 0.0
    lower = 0.0
    for axis in range(3):
        back = centre - shifted(axis, -1)
        front = shifted(axis, 1) - centre
        upper = upper + jnp.maximum(jnp.maximum(back, 0.0) ** 2, jnp.minimum(front, 0.0) ** 2)
        lower = lower + jnp.maximum(jnp.minimum(back, 0.0) ** 2, jnp.maximum(front, 0.0) ** 2)
    return -sign * (jnp.sqrt(jnp.where(sign >= 0.0, upper, lower)) - 1.0)

def periodic(field):

    def shifted(axis, offset):
        return jnp.roll(field, -offset, axis)
    return shifted

def reference(level_set, band_mask, rows, row_owner, row_tile):
    owner = row_owner[:, 0]
    grid_x = owner // N_GY * CX + row_tile // CY
    grid_y = owner % N_GY * CY + row_tile % CY
    velocity = jnp.zeros((NX, NY, NZ), jnp.float32).at[grid_x, grid_y].add(rows)
    speed = band_mask.astype(jnp.float32)[:, :, None] * velocity
    field = level_set
    for step in range(STEPS):
        first = field + TIME_STEP * hj_rate(periodic(field), speed)
        second = 0.75 * field + 0.25 * (first + TIME_STEP * hj_rate(periodic(first), speed))
        field = field / 3.0 + 2.0 / 3.0 * (second + TIME_STEP * hj_rate(periodic(second), speed))
    sign = field / jnp.sqrt(field * field + 1.0)
    for sweep in range(SWEEPS):
        field = field + PSEUDO_STEP * reinit_rate(periodic(field), field, sign)
    return field
```

```python
import functools

import jax
import jax.numpy as jnp
from jax import lax
from jax.experimental import pallas as pl
from jax.experimental.pallas import tpu as pltpu
from jax.sharding import PartitionSpec as P

EPSILON = 1e-06
TIME_STEP = 0.2
PSEUDO_STEP = 0.3

CX, CY, NZ = 64, 40, 128
DEVICES = 128
CAP = 16
SLOTS = CAP + 1
COLS = CX * CY

XO, YO = 12, 16
XR, YP = 88, 72
EXT = XR * YP
SPEED_HALO = 8
VMEM_LIMIT = 40 * 1024 * 1024
F32 = jnp.float32


def rcp(x):
    return pl.reciprocal(x, approx=True)


def pair_weights(e_left, e_right, g):
    total = e_left + e_right
    twice = g + g
    common = g * g * (13.0 / 3.0) + EPSILON
    after = total + twice
    before = total - twice
    ip = rcp(common + after * after)
    it = rcp(common + total * total)
    im = rcp(common + before * before)
    return ip * ip, it * it * 6.0, im * im, total


def weight_after(e_left, e_right, g):
    low = e_left + e_right + (g + g)
    i = rcp(g * g * (13.0 / 3.0) + EPSILON + low * low)
    return i * i


def weight_before(e_left, e_right, g):
    low = e_left + e_right - (g + g)
    i = rcp(g * g * (13.0 / 3.0) + EPSILON + low * low)
    return i * i


def weight_centre(e_left, e_right, g):
    low = e_left + e_right
    i = rcp(g * g * (13.0 / 3.0) + EPSILON + low * low)
    return i * i * 6.0


def central(slope, g, total):
    base = slope + g * (1.0 / 6.0)
    half = total * 0.5
    return base + half, half - base


def face_values(p1, p2, p3, h_left, h_right, q_left, q_right):
    low = p1 * h_left
    high = p3 * h_right
    both = p1 + p3 + p2
    left = q_left - (high + low * (2.0 / 3.0)) * rcp(both + (p3 + p3))
    right = q_right - (low + high * (2.0 / 3.0)) * rcp(both + (p1 + p1))
    return left, right


def upwind(sign, left, right):
    top = jnp.maximum(jnp.maximum(sign * left, sign * right), 0.0)
    return top * top


def sign_of(speed):
    return jnp.where(speed >= 0.0, 1.0, -1.0)


def root(x):
    return x * lax.rsqrt(jnp.maximum(x, 1e-37))


def prev_z(x):
    return pltpu.roll(x, 1, 1)


def next_z(x):
    return pltpu.roll(x, NZ - 1, 1)


def z_term(u, sign):
    e = 0.5 * (next_z(u) - u) - 0.5 * (u - prev_z(u))
    e_prev, e_next, e_after = prev_z(e), next_z(e), pltpu.roll(e, NZ - 2, 1)
    d = next_z(u) - u
    g_prev, g, g_next = e - e_prev, e_next - e, e_after - e_next
    h, h_next = g - g_prev, g_next - g
    pp = weight_after(e_prev, e, g_prev)
    pt = weight_centre(e, e_next, g)
    pm = weight_before(e_next, e_after, g_next)
    q_left, q_right = central(d, g, e + e_next)
    left, right = face_values(pp, pt, pm, h, h_next, q_left, q_right)
    return upwind(sign, prev_z(left), right)


def y_terms(u, signs):
    n = len(u) - 6
    out = []
    d_prev = u[1] - u[0]
    half_prev = 0.5 * d_prev
    d, e, g, h, pp, pt, pm, q, left = {}, {}, {}, {}, {}, {}, {}, {}, {}
    for k in range(1, n + 5):
        d[k] = u[k + 1] - u[k]
        half = 0.5 * d[k]
        e[k] = half - half_prev
        half_prev = half
        if k >= 2:
            f = k - 1
            g[f] = e[k] - e[f]
            ppf, ptf, pmf, total = pair_weights(e[f], e[k], g[f])
            pp[f], pt[f], pm[f] = ppf, ptf, pmf
            q[f] = central(d[f], g[f], total)
            if f >= 2:
                h[f] = g[f] - g[f - 1]
            if f >= 3:
                w = f - 1
                lw, rw = face_values(pp[w - 1], pt[w], pm[w + 1], h[w], h[w + 1], *q[w])
                left[w] = lw
                if w >= 3:
                    out.append(upwind(signs[w - 3], left[w - 1], rw))
    return out


def stage(src, speed, term, ny, x_lo, x_hi, y_lo, finish):
    group = 4
    unroll = (x_hi - x_lo) // group

    def tile(ref, x, j):
        return ref[pl.ds(x * YP + (y_lo + j), 8, stride=ny), :]

    def y_body(i, carry):
        for k in range(group):
            x = x_lo + i * group + k
            signs = [sign_of(tile(speed, x, j)) for j in range(ny)]
            u = [tile(src, x, j) for j in range(-3, ny + 3)]
            for j, value in enumerate(y_terms(u, signs)):
                term[pl.ds(pl.multiple_of(x * (8 * ny) + 8 * j, 8), 8), :] = value + z_term(
                    u[j + 3], signs[j]
                )
        return carry

    lax.fori_loop(0, (x_hi - x_lo) // group, y_body, 0)

    def advance(x, j, state):
        d, half, e, g, h, pp0, pp1, p2, ql, qr, left = state
        d2 = tile(src, x + 3, j) - tile(src, x + 2, j)
        half2 = 0.5 * d2
        e2 = half2 - half
        g2 = e2 - e
        pp2, pt2, pm2, total = pair_weights(e, e2, g2)
        ql2, qr2 = central(d, g2, total)
        h2 = g2 - g
        left2, right = face_values(pp0, p2, pm2, h, h2, ql, qr)
        return left, right, (d2, half2, e2, g2, h2, pp1, pp2, pt2, ql2, qr2, left2)

    def column(j, carry):
        zero = jnp.zeros((8, NZ), F32)
        x = x_lo - 1
        u = [tile(src, x + k, j) for k in range(-2, 3)]
        ds = [u[k + 1] - u[k] for k in range(4)]
        es = [0.5 * ds[k + 1] - 0.5 * ds[k] for k in range(3)]
        g0, g1 = es[1] - es[0], es[2] - es[1]
        ppa, _, _, _ = pair_weights(es[0], es[1], g0)
        ppb, ptb, _, total = pair_weights(es[1], es[2], g1)
        ql, qr = central(ds[2], g1, total)
        state = (ds[3], 0.5 * ds[3], es[2], g1, g1 - g0, ppa, ppb, ptb, ql, qr, zero)
        _, _, state = advance(x, j, state)

        def body(i, state):
            for k in range(unroll):
                x = x_lo + i * unroll + k
                left, right, state = advance(x, j, state)
                sp = tile(speed, x, j)
                sign = sign_of(sp)
                u0 = tile(src, x, j)
                total = (
                    upwind(sign, left, right)
                    + term[pl.ds(pl.multiple_of(x * (8 * ny) + 8 * j, 8), 8), :]
                )
                finish(x, j, u0, u0 - TIME_STEP * sp * root(total))
            return state

        lax.fori_loop(0, (x_hi - x_lo) // unroll, body, state)
        return carry

    lax.fori_loop(0, ny, column, 0)


def fill_block(ext, own, before, after, width):
    def put(src, x_to, count):
        def body(x, carry):
            for i in range(CY // 8):
                ext[pl.ds(pl.multiple_of((x + x_to) * YP + (YO + 8 * i), 8), 8), :] = src[
                    pl.ds(pl.multiple_of(x * CY + 8 * i, 8), 8), :
                ]
            return carry

        lax.fori_loop(0, count, body, 0)

    put(own, XO, CX)
    put(before, XO - width, width)
    put(after, XO + CX, width)


def fill_sides(ext, before, after, width):
    for t in range(width):
        for b in range(XR // 8):
            ext[pl.ds(b * 8 * YP + (YO - width + t), 8, stride=YP), :] = before[
                pl.ds(t * XR + 8 * b, 8), :
            ]
            ext[pl.ds(b * 8 * YP + (YO + CY + t), 8, stride=YP), :] = after[
                pl.ds(t * XR + 8 * b, 8), :
            ]


def sides_kernel(width, own, before, after, low, high, ext):
    fill_block(ext, own, before, after, width)
    for t in range(width):
        for b in range(XR // 8):
            low[pl.ds(t * XR + 8 * b, 8), :] = ext[pl.ds(b * 8 * YP + (YO + t), 8, stride=YP), :]
            high[pl.ds(t * XR + 8 * b, 8), :] = ext[
                pl.ds(b * 8 * YP + (YO + CY - width + t), 8, stride=YP), :
            ]


def params():
    return pltpu.CompilerParams(vmem_limit_bytes=VMEM_LIMIT)


def shape(rows):
    return jax.ShapeDtypeStruct((rows, NZ), F32)


def vmem(rows):
    return pltpu.VMEM((rows, NZ), F32)


def shift_pair(low, high, axis):
    size = lax.axis_size(axis)
    up = [(i, (i + 1) % size) for i in range(size)]
    down = [(j, i) for i, j in up]
    return lax.ppermute(high, axis, up), lax.ppermute(low, axis, down)


def halo(own, low, high, width):
    before, after = shift_pair(low, high, "gx")
    side_low, side_high = pl.pallas_call(
        functools.partial(sides_kernel, width),
        out_shape=(shape(width * XR), shape(width * XR)),
        scratch_shapes=[vmem(EXT)],
        compiler_params=params(),
        name="sides",
    )(own, before, after)
    left, right = shift_pair(side_low, side_high, "gy")
    return own, before, after, left, right


def store_tile(ref, x, j, ny, y_lo, value):
    ref[pl.ds(x * YP + (y_lo + j), 8, stride=ny), :] = value


def load_tile(ref, x, j, ny, y_lo):
    return ref[pl.ds(x * YP + (y_lo + j), 8, stride=ny), :]


def runge_kutta(width, next_width, make_speed, *refs):
    refs = list(refs)
    own, before, after, left, right = refs[:5]
    refs = refs[5:]
    if make_speed:
        s_own, s_before, s_after, s_left, s_right = refs[:5]
        refs = refs[5:]
    else:
        speed = refs.pop(0)
    out = refs.pop(0)
    if next_width:
        out_low, out_high = refs[:2]
        refs = refs[2:]
    if make_speed:
        speed = refs.pop(0)
    base, first, second, term = refs[:4]

    fill_block(base, own, before, after, width)
    fill_sides(base, left, right, width)
    if make_speed:
        fill_block(speed, s_own, s_before, s_after, SPEED_HALO)
        fill_sides(speed, s_left, s_right, SPEED_HALO)

    last = width - 9
    geometry = []
    for margin in (width - 3, width - 6, last):
        ny = (CY + 2 * margin + 7) // 8
        count = (CX + 2 * margin + 3) // 4 * 4
        geometry.append((ny, XO - margin, XO - margin + count, YO - margin))

    ny, x_lo, x_hi, y_lo = geometry[0]

    def finish_one(x, j, u, moved):
        store_tile(first, x, j, geometry[0][0], geometry[0][3], moved)

    stage(base, speed, term, ny, x_lo, x_hi, y_lo, finish_one)

    ny2, x_lo2, x_hi2, y_lo2 = geometry[1]

    def finish_two(x, j, u, moved):
        store_tile(
            second, x, j, ny2, y_lo2, 0.75 * load_tile(base, x, j, ny2, y_lo2) + 0.25 * moved
        )

    stage(first, speed, term, ny2, x_lo2, x_hi2, y_lo2, finish_two)

    ny3, x_lo3, x_hi3, y_lo3 = geometry[2]

    def finish_three(x, j, u, moved):
        value = (1.0 / 3.0) * load_tile(base, x, j, ny3, y_lo3) + (2.0 / 3.0) * moved
        if next_width:
            out[pl.ds((x - XO) * CY + j, 8, stride=ny3), :] = value
        else:
            store_tile(first, x, j, ny3, y_lo3, value)

    stage(second, speed, term, ny3, x_lo3, x_hi3, y_lo3, finish_three)

    if next_width:
        rows = next_width * CY
        out_low[...] = out[pl.ds(0, rows), :]
        out_high[...] = out[pl.ds(COLS - rows, rows), :]
        return

    def sweep(src, margin, store):
        ny = (CY + 2 * margin + 7) // 8
        y_lo = YO - margin

        def body(x, carry):
            u = [load_tile(src, x, j, ny, y_lo) for j in range(-1, ny + 1)]
            for j in range(ny):
                v = u[j + 1]
                advected = load_tile(first, x, j, ny, y_lo)
                sign = sign_of(advected)
                total = upwind(sign, v - u[j], v - u[j + 2])
                total += upwind(
                    sign,
                    v - load_tile(src, x - 1, j, ny, y_lo),
                    v - load_tile(src, x + 1, j, ny, y_lo),
                )
                total += upwind(sign, v - prev_z(v), v - next_z(v))
                smooth = advected * lax.rsqrt(advected * advected + 1.0)
                store(x, j, ny, y_lo, v - PSEUDO_STEP * smooth * (root(total) - 1.0))
            return carry

        lax.fori_loop(XO - margin, XO + CX + margin, body, 0)

    sweep(first, 1, lambda x, j, ny, y_lo, v: store_tile(second, x, j, ny, y_lo, v))

    def store_out(x, j, ny, y_lo, v):
        out[pl.ds((x - XO) * CY + j, 8, stride=ny), :] = v

    sweep(second, 0, store_out)


def step_call(width, next_width, pieces, speed):
    make_speed = isinstance(speed, tuple)
    outs = [shape(COLS)]
    if next_width:
        outs += [shape(next_width * CY)] * 2
    if make_speed:
        outs += [shape(EXT)]
        operands = (*pieces, *speed)
    else:
        operands = (*pieces, speed)
    return pl.pallas_call(
        functools.partial(runge_kutta, width, next_width, make_speed),
        out_shape=tuple(outs),
        scratch_shapes=[vmem(EXT), vmem(EXT), vmem(EXT), vmem(XR * 56)],
        compiler_params=params(),
        name="step",
    )(*operands)


def split(x):
    high = x.astype(jnp.bfloat16)
    low = (x - high.astype(F32)).astype(jnp.bfloat16)
    return jnp.concatenate([high, low], axis=1)


def onehot(mask):
    return jnp.where(mask, 1.0, 0.0).astype(jnp.bfloat16)


def pack_kernel(rows, owner, column, send, parts):
    count = rows.shape[0]
    own = owner[...]
    tags = onehot(lax.broadcasted_iota(jnp.int32, (DEVICES, count), 0) == own)
    order = onehot(
        lax.broadcasted_iota(jnp.int32, (count, count), 0)
        < lax.broadcasted_iota(jnp.int32, (count, count), 1)
    )
    earlier = jnp.dot(tags, order, preferred_element_type=F32)
    rank = jnp.sum(earlier * tags.astype(F32), axis=0, keepdims=True).astype(jnp.int32)
    target = own * SLOTS + rank
    parts[...] = split(rows[...])

    block = 128

    def body(b, carry):
        slot = lax.broadcasted_iota(jnp.int32, (block, count), 0) + b * block
        both = jnp.dot(onehot(slot == target), parts[...], preferred_element_type=F32)
        send[pl.ds(pl.multiple_of(b * block, block), block), :] = both[:, :NZ] + both[:, NZ:]
        return carry

    lax.fori_loop(0, DEVICES * SLOTS // block, body, 0)

    place = lax.broadcasted_iota(jnp.int32, (NZ, count), 0) == rank
    number = column[...] + 1
    dims = (((1,), (1,)), ((), ()))
    total = jnp.zeros((DEVICES, NZ), F32)
    for part, scale in ((number >> 6, 64.0), (number & 63, 1.0)):
        held = jnp.where(place, part.astype(F32), 0.0).astype(jnp.bfloat16)
        total += scale * lax.dot_general(tags, held, dims, preferred_element_type=F32)
    for b in range(DEVICES // 8):
        send[pl.ds(b * 8 * SLOTS + CAP, 8, stride=SLOTS), :] = total[8 * b : 8 * b + 8]


def unpack_kernel(low_rows, got, mask, speed, speed_low, speed_high, parts, number):
    for b in range(DEVICES // 8):
        number[pl.ds(8 * b, 8), :] = got[pl.ds(b * 8 * SLOTS + CAP, 8, stride=SLOTS), :]
    columns = number[...].T.astype(jnp.int32) - 1
    for k in range(CAP):
        for b in range(DEVICES // 16):
            pair = [
                got[pl.ds((b * 16 + 8 * i) * SLOTS + k, 8, stride=SLOTS), :] for i in range(2)
            ]
            parts[pl.ds(k * DEVICES + 16 * b, 16), :] = split(jnp.concatenate(pair, axis=0))
    named = jnp.concatenate([columns[k : k + 1, :] for k in range(CAP)], axis=1)

    block = 128

    def body(b, carry):
        cell = lax.broadcasted_iota(jnp.int32, (block, CAP * DEVICES), 0) + b * block
        both = jnp.dot(onehot(cell == named), parts[...], preferred_element_type=F32)
        at = pl.ds(pl.multiple_of(b * block, block), block)
        speed[at, :] = (both[:, :NZ] + both[:, NZ:]) * mask[at, :]
        return carry

    lax.fori_loop(0, COLS // block, body, 0)
    speed_low[...] = speed[pl.ds(0, low_rows), :]
    speed_high[...] = speed[pl.ds(COLS - low_rows, low_rows), :]


def shards(level_set, band_mask, rows, row_owner, row_tile):
    count = rows.shape[0]
    send = pl.pallas_call(
        pack_kernel,
        out_shape=shape(DEVICES * SLOTS),
        scratch_shapes=[pltpu.VMEM((count, 2 * NZ), jnp.bfloat16)],
        compiler_params=params(),
        name="pack",
    )(rows, row_owner.reshape(1, count), row_tile.reshape(1, count))
    got = lax.all_to_all(send, ("gx", "gy"), split_axis=0, concat_axis=0, tiled=True)

    u = level_set.reshape(COLS, NZ)
    pieces = halo(u, u[: 9 * CY], u[COLS - 9 * CY :], 9)

    mask = band_mask.astype(F32).reshape(COLS, 1)
    face = SPEED_HALO * CY
    speed, speed_low, speed_high = pl.pallas_call(
        functools.partial(unpack_kernel, face),
        out_shape=(shape(COLS), shape(face), shape(face)),
        scratch_shapes=[pltpu.VMEM((CAP * DEVICES, 2 * NZ), jnp.bfloat16), vmem(DEVICES)],
        compiler_params=params(),
        name="unpack",
    )(got, mask)
    speed_pieces = halo(speed, speed_low, speed_high, SPEED_HALO)

    u, low, high, speed = step_call(9, 9, pieces, speed_pieces)
    u, low, high = step_call(9, 11, halo(u, low, high, 9), speed)
    (u,) = step_call(11, 0, halo(u, low, high, 11), speed)
    return u.reshape(CX, CY, NZ)


def solution(mesh):
    return jax.shard_map(
        shards,
        mesh=mesh,
        in_specs=(
            P("gx", "gy", None),
            P("gx", "gy"),
            P(("gx", "gy"), None),
            P(("gx", "gy"), None),
            P(("gx", "gy")),
        ),
        out_specs=P("gx", "gy", None),
        check_vma=False,
    )
```

```python
import functools

import jax
import jax.numpy as jnp
from jax import lax
from jax.experimental import pallas as pl
from jax.experimental.pallas import tpu as pltpu
from jax.sharding import PartitionSpec as P

EPSILON = 1e-06
TIME_STEP = 0.2
PSEUDO_STEP = 0.3

CX, CY, NZ = 64, 40, 128
DEVICES = 128
CAP = 16
SLOTS = CAP + 1
COLS = CX * CY

XO, YO = 12, 16
XR, YP = 88, 72
EXT = XR * YP
SPEED_HALO = 8
VMEM_LIMIT = 40 * 1024 * 1024
F32 = jnp.float32


def rcp(x):
    return pl.reciprocal(x, approx=True)


QUARTER = 0.25 * EPSILON


def pair_weights(e_left, e_right, g):
    total = e_left + e_right
    half = 0.5 * total
    square = g * g
    centre = half * half + (square * (13.0 / 12.0) + QUARTER)
    ends = centre + square
    cross = total * g
    ip = rcp(ends + cross)
    it = rcp(centre)
    im = rcp(ends - cross)
    return ip * ip, it * it * 3.0, im * im, half


def weight_end(half, g):
    i = rcp(half * half + (g * g * (13.0 / 12.0) + QUARTER))
    return i * i


def central(slope, sixth, half):
    base = slope + sixth
    return base + half, half - base


def face_values(p1, p2, p3, h_left, h_right, q_left, q_right):
    low = p1 * h_left
    high = p3 * h_right
    both = 0.5 * (p1 + p3) + p2
    twice = low + high
    twice = twice + twice
    left = q_left - (twice + high) * rcp(both + p3)
    right = q_right - (twice + low) * rcp(both + p1)
    return left, right


def upwind(sign, left, right):
    top = jnp.maximum(jnp.maximum(sign * left, sign * right), 0.0)
    return top * top


def sign_of(value):
    return jnp.where(value >= 0.0, 1.0, -1.0)


def speed_sign(pace):
    return jnp.where(pace <= 0.0, 1.0, -1.0)


def root(x):
    return x * lax.rsqrt(jnp.maximum(x, 1e-37))


def prev_z(x):
    return pltpu.roll(x, 1, 1)


def next_z(x):
    return pltpu.roll(x, NZ - 1, 1)


def z_slopes(u):
    after = next_z(u)
    return after - u, 0.5 * (after + prev_z(u)) - u


def z_faces(d, e):
    e_prev, e_next, e_after = prev_z(e), next_z(e), pltpu.roll(e, NZ - 2, 1)
    g_prev, g, g_next = e - e_prev, e_next - e, e_after - e_next
    sixth = g * (1.0 / 6.0)
    h = sixth - g_prev * (1.0 / 6.0)
    h_next = g_next * (1.0 / 6.0) - sixth
    half = 0.5 * (e + e_next)
    pp = weight_end(0.5 * (e_prev + e) + g_prev, g_prev)
    pt = weight_end(half, g) * 3.0
    pm = weight_end(0.5 * (e_next + e_after) - g_next, g_next)
    return face_values(pp, pt, pm, h, h_next, *central(d, sixth, half))


def y_terms(u, signs):
    n = len(u) - 6
    out = []
    d, e, sixth, h, pp, pt, pm, q, left = {}, {}, {}, {}, {}, {}, {}, {}, {}
    d[0] = u[1] - u[0]
    for k in range(1, n + 5):
        d[k] = u[k + 1] - u[k]
        e[k] = 0.5 * (d[k] - d[k - 1])
        if k >= 2:
            f = k - 1
            g = e[k] - e[f]
            sixth[f] = g * (1.0 / 6.0)
            pp[f], pt[f], pm[f], half = pair_weights(e[f], e[k], g)
            q[f] = central(d[f], sixth[f], half)
            if f >= 2:
                h[f] = sixth[f] - sixth[f - 1]
            if f >= 3:
                w = f - 1
                lw, rw = face_values(pp[w - 1], pt[w], pm[w + 1], h[w], h[w + 1], *q[w])
                left[w] = lw
                if w >= 3:
                    out.append(upwind(signs[w - 3], left[w - 1], rw))
    return out


GROUP = 4


def geometry(width, margin):
    count = (CX + 2 * margin + GROUP - 1) // GROUP * GROUP
    return ((CY + 2 * margin + 7) // 8, XO - margin, XO - margin + count, YO - margin)


def load_tile(ref, geo, x, j):
    return ref[pl.ds(x * YP + (geo[3] + j), 8, stride=geo[0]), :]


def store_tile(ref, geo, x, j, value):
    ref[pl.ds(x * YP + (geo[3] + j), 8, stride=geo[0]), :] = value


def store_slopes(slopes, geo, x, j, value):
    d, e = z_slopes(value)
    store_tile(slopes[0], geo, x, j, d)
    store_tile(slopes[1], geo, x, j, e)


def packed(geo, x, j):
    return pl.ds(pl.multiple_of(x * (8 * geo[0]) + 8 * j, 8), 8)


def over_rows(geo, row):
    def body(i, carry):
        for k in range(GROUP):
            row(geo[1] + i * GROUP + k)
        return carry

    lax.fori_loop(0, (geo[2] - geo[1]) // GROUP, body, 0)


def z_row(slopes, faces, geo, x, j):
    left, right = z_faces(load_tile(slopes[0], geo, x, j), load_tile(slopes[1], geo, x, j))
    faces[0][packed(geo, x, j), :] = left
    faces[1][packed(geo, x, j), :] = right


def y_pass(src, pace, geo, emit):
    ny = geo[0]

    def row(x):
        paces = [load_tile(pace, geo, x, j) for j in range(ny)]
        u = [load_tile(src, geo, x, j) for j in range(-3, ny + 3)]
        for j, value in enumerate(y_terms(u, [speed_sign(p) for p in paces])):
            emit(x, j, u[j + 3], paces[j], value)

    over_rows(geo, row)


def x_pass(src, pace, faces, geo, emit):
    ny, x_lo, x_hi, _ = geo
    unroll = (x_hi - x_lo) // 4

    def tile(x, j):
        return load_tile(src, geo, x, j)

    def advance(x, j, state):
        d, e, sixth, g, h, pp0, pp1, p2, ql, qr, left = state
        d2 = tile(x + 3, j) - tile(x + 2, j)
        e2 = 0.5 * (d2 - d)
        g2 = e2 - e
        sixth2 = g2 * (1.0 / 6.0)
        pp2, pt2, pm2, half = pair_weights(e, e2, g2)
        ql2, qr2 = central(d, sixth2, half)
        h2 = sixth2 - sixth
        left2, right = face_values(pp0, p2, pm2, h, h2, ql, qr)
        return left, right, (d2, e2, sixth2, g2, h2, pp1, pp2, pt2, ql2, qr2, left2)

    def column(j, carry):
        zero = jnp.zeros((8, NZ), F32)
        x = x_lo - 1
        u = [tile(x + k, j) for k in range(-2, 3)]
        ds = [u[k + 1] - u[k] for k in range(4)]
        es = [0.5 * (ds[k + 1] - ds[k]) for k in range(3)]
        g0, g1 = es[1] - es[0], es[2] - es[1]
        ppa, _, _, _ = pair_weights(es[0], es[1], g0)
        ppb, ptb, _, half = pair_weights(es[1], es[2], g1)
        s0, s1 = g0 * (1.0 / 6.0), g1 * (1.0 / 6.0)
        ql, qr = central(ds[2], s1, half)
        state = (ds[3], es[2], s1, g1, s1 - s0, ppa, ppb, ptb, ql, qr, zero)
        _, _, state = advance(x, j, state)

        def body(i, state):
            for k in range(unroll):
                x = x_lo + i * unroll + k
                left, right, state = advance(x, j, state)
                p = load_tile(pace, geo, x, j)
                sign = speed_sign(p)
                at = packed(geo, x, j)
                total = upwind(sign, left, right) + upwind(
                    sign, prev_z(faces[0][at, :]), faces[1][at, :]
                )
                emit(x, j, tile(x, j), p, total)
            return state

        lax.fori_loop(0, 4, body, state)
        return carry

    lax.fori_loop(0, ny, column, 0)


def stage(src, slopes, pace, term, faces, geo, finish):
    def keep(x, j, u, p, value):
        term[packed(geo, x, j), :] = value
        z_row(slopes, faces, geo, x, j)

    def join(x, j, u, p, value):
        finish(x, j, u, u + p * root(value + term[packed(geo, x, j), :]))

    y_pass(src, pace, geo, keep)
    x_pass(src, pace, faces, geo, join)


def fill_block(ext, own, before, after, width, slopes=None):
    def put(src, x_to, count, group):
        def body(n, carry):
            for k in range(group):
                x = n * group + k
                for i in range(CY // 8):
                    value = src[pl.ds(pl.multiple_of(x * CY + 8 * i, 8), 8), :]
                    at = pl.ds(pl.multiple_of((x + x_to) * YP + (YO + 8 * i), 8), 8)
                    ext[at, :] = value
                    if slopes:
                        slopes[0][at, :], slopes[1][at, :] = z_slopes(value)
            return carry

        lax.fori_loop(0, count // group, body, 0)

    put(own, XO, CX, 8)
    put(before, XO - width, width, width)
    put(after, XO + CX, width, width)


def fill_sides(ext, before, after, width, slopes=None):
    for t in range(width):
        for b in range(XR // 8):
            for src, y in ((before, YO - width + t), (after, YO + CY + t)):
                value = src[pl.ds(t * XR + 8 * b, 8), :]
                at = pl.ds(b * 8 * YP + y, 8, stride=YP)
                ext[at, :] = value
                if slopes:
                    slopes[0][at, :], slopes[1][at, :] = z_slopes(value)


def sides_kernel(width, own, before, after, low, high, ext):
    fill_block(ext, own, before, after, width)
    for t in range(width):
        for b in range(XR // 8):
            low[pl.ds(t * XR + 8 * b, 8), :] = ext[pl.ds(b * 8 * YP + (YO + t), 8, stride=YP), :]
            high[pl.ds(t * XR + 8 * b, 8), :] = ext[
                pl.ds(b * 8 * YP + (YO + CY - width + t), 8, stride=YP), :
            ]


def params():
    return pltpu.CompilerParams(vmem_limit_bytes=VMEM_LIMIT)


def shape(rows):
    return jax.ShapeDtypeStruct((rows, NZ), F32)


def vmem(rows):
    return pltpu.VMEM((rows, NZ), F32)


def shift_pair(low, high, axis):
    size = lax.axis_size(axis)
    up = [(i, (i + 1) % size) for i in range(size)]
    down = [(j, i) for i, j in up]
    return lax.ppermute(high, axis, up), lax.ppermute(low, axis, down)


def cross_x(own, low, high, width):
    before, after = shift_pair(low, high, "gx")
    side_low, side_high = pl.pallas_call(
        functools.partial(sides_kernel, width),
        out_shape=(shape(width * XR), shape(width * XR)),
        scratch_shapes=[vmem(EXT)],
        compiler_params=params(),
        cost_estimate=cost(1),
        name="sides",
    )(own, before, after)
    return (own, before, after), (side_low, side_high)


def cost(us):
    return pl.CostEstimate(
        flops=1000 * us, bytes_accessed=int(3.0e6 * us), transcendentals=0
    )


def own_geometry(width):
    _, x_lo, x_hi, _ = geometry(width, width - 3)
    return (CY // 8, x_lo, x_hi, YO)


def early_kernel(width, pace_ready, *refs):
    refs = list(refs)
    own, before, after = refs[:3]
    refs = refs[3:]
    if pace_ready:
        pace = refs.pop(0)
    else:
        p_own, p_before, p_after = refs[:3]
        refs = refs[3:]
    out, base = refs[:2]
    slopes, faces = refs[2:4], refs[4:6]
    if not pace_ready:
        pace = refs[6]
        fill_block(pace, p_own, p_before, p_after, SPEED_HALO)
    fill_block(base, own, before, after, width, slopes)
    geo = own_geometry(width)

    def row(x):
        for j in range(geo[0]):
            z_row(slopes, faces, geo, x, j)

    over_rows(geo, row)

    def emit(x, j, u, p, value):
        out[packed(geo, x, j), :] = value

    x_pass(base, pace, faces, geo, emit)


def early_call(width, pieces, pace):
    ready = not isinstance(pace, tuple)
    return pl.pallas_call(
        functools.partial(early_kernel, width, ready),
        out_shape=shape(XR * CY),
        scratch_shapes=[vmem(EXT)] * 3
        + [vmem(XR * CY)] * 2
        + ([] if ready else [vmem(EXT)]),
        compiler_params=params(),
        cost_estimate=cost(10),
        name="early",
    )(*pieces, *((pace,) if ready else pace))


def runge_kutta(width, next_width, make_pace, *refs):
    refs = list(refs)
    own, before, after, left, right, early = refs[:6]
    refs = refs[6:]
    if make_pace:
        p_own, p_before, p_after, p_left, p_right = refs[:5]
        refs = refs[5:]
    else:
        pace = refs.pop(0)
    out = refs.pop(0)
    if next_width:
        out_low, out_high = refs[:2]
        refs = refs[2:]
    if make_pace:
        pace = refs.pop(0)
    base, first, second = refs[:3]
    even, odd, term, faces = refs[3:5], refs[5:7], refs[7], refs[8:10]

    fill_block(base, own, before, after, width)
    fill_sides(base, left, right, width, even)
    if make_pace:
        fill_block(pace, p_own, p_before, p_after, SPEED_HALO)
        fill_sides(pace, p_left, p_right, SPEED_HALO)

    def finish_one(geo):
        def finish(x, j, u, moved):
            store_tile(first, geo, x, j, moved)
            store_slopes(odd, geo, x, j, moved)

        return finish

    inner = own_geometry(width)
    done = finish_one(inner)

    def join(x, j, u, p, value):
        done(x, j, u, u + p * root(value + early[packed(inner, x, j), :]))

    y_pass(base, pace, inner, join)
    for y_lo in (YO - 8, YO + CY):
        side = (1, inner[1], inner[2], y_lo)
        stage(base, even, pace, term, faces, side, finish_one(side))

    geo2 = geometry(width, width - 6)

    def finish_two(x, j, u, moved):
        value = 0.75 * load_tile(base, geo2, x, j) + 0.25 * moved
        store_tile(second, geo2, x, j, value)
        store_slopes(even, geo2, x, j, value)

    stage(first, odd, pace, term, faces, geo2, finish_two)

    geo3 = geometry(width, width - 9)

    def finish_three(x, j, u, moved):
        value = (1.0 / 3.0) * load_tile(base, geo3, x, j) + (2.0 / 3.0) * moved
        if next_width:
            out[pl.ds((x - XO) * CY + j, 8, stride=geo3[0]), :] = value
        else:
            store_tile(first, geo3, x, j, value)

    stage(second, even, pace, term, faces, geo3, finish_three)

    if next_width:
        rows = next_width * CY
        out_low[...] = out[pl.ds(0, rows), :]
        out_high[...] = out[pl.ds(COLS - rows, rows), :]
        return

    def sweep(src, geo, store):
        ny = geo[0]

        def row(x):
            u = [load_tile(src, geo, x, j) for j in range(-1, ny + 1)]
            for j in range(ny):
                v = u[j + 1]
                advected = load_tile(first, geo, x, j)
                sign = sign_of(advected)
                total = upwind(sign, v - u[j], v - u[j + 2])
                total += upwind(
                    sign,
                    v - load_tile(src, geo, x - 1, j),
                    v - load_tile(src, geo, x + 1, j),
                )
                total += upwind(sign, v - prev_z(v), v - next_z(v))
                smooth = advected * lax.rsqrt(advected * advected + 1.0)
                store(x, j, v - PSEUDO_STEP * smooth * (root(total) - 1.0))

        over_rows(geo, row)

    wide, block = geometry(width, 1), geometry(width, 0)
    sweep(first, wide, lambda x, j, v: store_tile(second, wide, x, j, v))

    def store_out(x, j, v):
        out[pl.ds((x - XO) * CY + j, 8, stride=block[0]), :] = v

    sweep(second, block, store_out)


def step_call(width, next_width, pieces, early, pace):
    make_pace = isinstance(pace, tuple)
    outs = [shape(COLS)]
    if next_width:
        outs += [shape(next_width * CY)] * 2
    if make_pace:
        outs += [shape(EXT)]
    return pl.pallas_call(
        functools.partial(runge_kutta, width, next_width, make_pace),
        out_shape=tuple(outs),
        scratch_shapes=[vmem(EXT)] * 7 + [vmem(XR * 56)] * 3,
        compiler_params=params(),
        cost_estimate=cost(35),
        name="step",
    )(*pieces, early, *(pace if make_pace else (pace,)))


def split(x):
    high = x.astype(jnp.bfloat16)
    low = (x - high.astype(F32)).astype(jnp.bfloat16)
    return jnp.concatenate([high, low], axis=1)


def onehot(mask):
    return jnp.where(mask, 1.0, 0.0).astype(jnp.bfloat16)


def pack_kernel(rows, owner, column, send, parts):
    count = rows.shape[0]
    own = owner[...]
    tags = onehot(lax.broadcasted_iota(jnp.int32, (DEVICES, count), 0) == own)
    order = onehot(
        lax.broadcasted_iota(jnp.int32, (count, count), 0)
        < lax.broadcasted_iota(jnp.int32, (count, count), 1)
    )
    earlier = jnp.dot(tags, order, preferred_element_type=F32)
    rank = jnp.sum(earlier * tags.astype(F32), axis=0, keepdims=True).astype(jnp.int32)
    target = own * SLOTS + rank
    parts[...] = split(rows[...])

    block = 128

    def body(b, carry):
        slot = lax.broadcasted_iota(jnp.int32, (block, count), 0) + b * block
        both = jnp.dot(onehot(slot == target), parts[...], preferred_element_type=F32)
        send[pl.ds(pl.multiple_of(b * block, block), block), :] = both[:, :NZ] + both[:, NZ:]
        return carry

    lax.fori_loop(0, DEVICES * SLOTS // block, body, 0)

    place = lax.broadcasted_iota(jnp.int32, (NZ, count), 0) == rank
    number = column[...] + 1
    dims = (((1,), (1,)), ((), ()))
    total = jnp.zeros((DEVICES, NZ), F32)
    for part, scale in ((number >> 6, 64.0), (number & 63, 1.0)):
        held = jnp.where(place, part.astype(F32), 0.0).astype(jnp.bfloat16)
        total += scale * lax.dot_general(tags, held, dims, preferred_element_type=F32)
    for b in range(DEVICES // 8):
        send[pl.ds(b * 8 * SLOTS + CAP, 8, stride=SLOTS), :] = total[8 * b : 8 * b + 8]


def unpack_kernel(low_rows, got, mask, speed, speed_low, speed_high, parts, number):
    for b in range(DEVICES // 8):
        number[pl.ds(8 * b, 8), :] = got[pl.ds(b * 8 * SLOTS + CAP, 8, stride=SLOTS), :]
    columns = number[...].T.astype(jnp.int32) - 1
    for k in range(CAP):
        for b in range(DEVICES // 16):
            pair = [
                got[pl.ds((b * 16 + 8 * i) * SLOTS + k, 8, stride=SLOTS), :] for i in range(2)
            ]
            parts[pl.ds(k * DEVICES + 16 * b, 16), :] = split(jnp.concatenate(pair, axis=0))
    named = jnp.concatenate([columns[k : k + 1, :] for k in range(CAP)], axis=1)

    block = 128

    def body(b, carry):
        cell = lax.broadcasted_iota(jnp.int32, (block, CAP * DEVICES), 0) + b * block
        both = jnp.dot(onehot(cell == named), parts[...], preferred_element_type=F32)
        at = pl.ds(pl.multiple_of(b * block, block), block)
        speed[at, :] = (both[:, :NZ] + both[:, NZ:]) * (mask[at, :] * -TIME_STEP)
        return carry

    lax.fori_loop(0, COLS // block, body, 0)
    speed_low[...] = speed[pl.ds(0, low_rows), :]
    speed_high[...] = speed[pl.ds(COLS - low_rows, low_rows), :]


def shards(level_set, band_mask, rows, row_owner, row_tile):
    count = rows.shape[0]
    send = pl.pallas_call(
        pack_kernel,
        out_shape=shape(DEVICES * SLOTS),
        scratch_shapes=[pltpu.VMEM((count, 2 * NZ), jnp.bfloat16)],
        compiler_params=params(),
        name="pack",
    )(rows, row_owner.reshape(1, count), row_tile.reshape(1, count))
    got = lax.all_to_all(send, ("gx", "gy"), split_axis=0, concat_axis=0, tiled=True)

    u = level_set.reshape(COLS, NZ)
    pieces, sides = cross_x(u, u[: 9 * CY], u[COLS - 9 * CY :], 9)
    pieces = (*pieces, *shift_pair(*sides, "gy"))
    got, pieces = lax.optimization_barrier((got, pieces))

    mask = band_mask.astype(F32).reshape(COLS, 1)
    face = SPEED_HALO * CY
    pace, pace_low, pace_high = pl.pallas_call(
        functools.partial(unpack_kernel, face),
        out_shape=(shape(COLS), shape(face), shape(face)),
        scratch_shapes=[pltpu.VMEM((CAP * DEVICES, 2 * NZ), jnp.bfloat16), vmem(DEVICES)],
        compiler_params=params(),
        cost_estimate=cost(6),
        name="unpack",
    )(got, mask)
    paces, sides = cross_x(pace, pace_low, pace_high, SPEED_HALO)
    early = early_call(9, pieces[:3], paces)
    paces = (*paces, *shift_pair(*sides, "gy"))
    u, low, high, pace = step_call(9, 9, pieces, early, paces)

    for width, next_width in ((9, 11), (11, 0)):
        pieces, sides = cross_x(u, low, high, width)
        early = early_call(width, pieces, pace)
        pieces = (*pieces, *shift_pair(*sides, "gy"))
        u, *faces = step_call(width, next_width, pieces, early, pace)
        low, high = faces or (None, None)
    return u.reshape(CX, CY, NZ)


def solution(mesh):
    return jax.shard_map(
        shards,
        mesh=mesh,
        in_specs=(
            P("gx", "gy", None),
            P("gx", "gy"),
            P(("gx", "gy"), None),
            P(("gx", "gy"), None),
            P(("gx", "gy")),
        ),
        out_specs=P("gx", "gy", None),
        check_vma=False,
    )
```

```python
import functools

import jax
import jax.numpy as jnp
from jax import lax
from jax.experimental import pallas as pl
from jax.experimental.pallas import tpu as pltpu
from jax.sharding import PartitionSpec as P

EPSILON = 1e-06
TIME_STEP = 0.2
PSEUDO_STEP = 0.3

CX, CY, NZ = 64, 40, 128
DEVICES = 128
CAP = 16
SLOTS = CAP + 1
COLS = CX * CY

XO, YO = 12, 16
XR, YP = 88, 72
EXT = XR * YP
SPEED_HALO = 8
VMEM_LIMIT = 40 * 1024 * 1024
F32 = jnp.float32


def rcp(x):
    return pl.reciprocal(x, approx=True)


QUARTER = 0.25 * EPSILON


def pair_weights(e_left, e_right, g):
    total = e_left + e_right
    half = 0.5 * total
    square = g * g
    centre = half * half + (square * (13.0 / 12.0) + QUARTER)
    ends = centre + square
    cross = total * g
    ip = rcp(ends + cross)
    it = rcp(centre)
    im = rcp(ends - cross)
    return ip * ip, it * it * 3.0, im * im, half


def weight_end(half, g):
    i = rcp(half * half + (g * g * (13.0 / 12.0) + QUARTER))
    return i * i


def central(slope, sixth, half):
    base = slope + sixth
    return base + half, half - base


def face_values(p1, p2, p3, h_left, h_right, q_left, q_right):
    low = p1 * h_left
    high = p3 * h_right
    both = 0.5 * (p1 + p3) + p2
    twice = low + high
    twice = twice + twice
    left = q_left - (twice + high) * rcp(both + p3)
    right = q_right - (twice + low) * rcp(both + p1)
    return left, right


def upwind(sign, left, right):
    top = jnp.maximum(jnp.maximum(sign * left, sign * right), 0.0)
    return top * top


def rise(left, right):
    top = jnp.maximum(jnp.maximum(left, right), 0.0)
    return top * top


def fall(left, right):
    top = jnp.minimum(jnp.minimum(left, right), 0.0)
    return top * top


def sign_of(value):
    return jnp.where(value >= 0.0, 1.0, -1.0)


def speed_sign(pace):
    return jnp.where(pace <= 0.0, 1.0, -1.0)


def root(x):
    return x * lax.rsqrt(jnp.maximum(x, 1e-37))


def prev_z(x):
    return pltpu.roll(x, 1, 1)


def next_z(x):
    return pltpu.roll(x, NZ - 1, 1)


def z_slopes(u):
    after = next_z(u)
    return after - u, 0.5 * (after + prev_z(u)) - u


def z_faces(d, e):
    e_prev, e_next, e_after = prev_z(e), next_z(e), pltpu.roll(e, NZ - 2, 1)
    g_prev, g, g_next = e - e_prev, e_next - e, e_after - e_next
    sixth = g * (1.0 / 6.0)
    h = sixth - g_prev * (1.0 / 6.0)
    h_next = g_next * (1.0 / 6.0) - sixth
    half = 0.5 * (e + e_next)
    pp = weight_end(0.5 * (e_prev + e) + g_prev, g_prev)
    pt = weight_end(half, g) * 3.0
    pm = weight_end(0.5 * (e_next + e_after) - g_next, g_next)
    return face_values(pp, pt, pm, h, h_next, *central(d, sixth, half))


def y_terms(u, signs):
    n = len(u) - 6
    out = []
    d, e, sixth, h, pp, pt, pm, q, left = {}, {}, {}, {}, {}, {}, {}, {}, {}
    d[0] = u[1] - u[0]
    for k in range(1, n + 5):
        d[k] = u[k + 1] - u[k]
        e[k] = 0.5 * (d[k] - d[k - 1])
        if k >= 2:
            f = k - 1
            g = e[k] - e[f]
            sixth[f] = g * (1.0 / 6.0)
            pp[f], pt[f], pm[f], half = pair_weights(e[f], e[k], g)
            q[f] = central(d[f], sixth[f], half)
            if f >= 2:
                h[f] = sixth[f] - sixth[f - 1]
            if f >= 3:
                w = f - 1
                lw, rw = face_values(pp[w - 1], pt[w], pm[w + 1], h[w], h[w + 1], *q[w])
                left[w] = lw
                if w >= 3:
                    out.append(upwind(signs[w - 3], left[w - 1], rw))
    return out


GROUP = 4


def geometry(width, margin):
    count = (CX + 2 * margin + GROUP - 1) // GROUP * GROUP
    return ((CY + 2 * margin + 7) // 8, XO - margin, XO - margin + count, YO - margin)


def load_tile(ref, geo, x, j):
    return ref[pl.ds(x * YP + (geo[3] + j), 8, stride=geo[0]), :]


def store_tile(ref, geo, x, j, value):
    ref[pl.ds(x * YP + (geo[3] + j), 8, stride=geo[0]), :] = value


def store_slopes(slopes, geo, x, j, value):
    d, e = z_slopes(value)
    store_tile(slopes[0], geo, x, j, d)
    store_tile(slopes[1], geo, x, j, e)


def packed(geo, x, j):
    return pl.ds(pl.multiple_of(x * (8 * geo[0]) + 8 * j, 8), 8)


def over_rows(geo, row):
    def body(i, carry):
        for k in range(GROUP):
            row(geo[1] + i * GROUP + k)
        return carry

    lax.fori_loop(0, (geo[2] - geo[1]) // GROUP, body, 0)


def z_row(slopes, faces, geo, x, j):
    left, right = z_faces(load_tile(slopes[0], geo, x, j), load_tile(slopes[1], geo, x, j))
    faces[0][packed(geo, x, j), :] = left
    faces[1][packed(geo, x, j), :] = right


def y_pass(src, pace, geo, emit):
    ny = geo[0]

    def row(x):
        paces = [load_tile(pace, geo, x, j) for j in range(ny)]
        u = [load_tile(src, geo, x, j) for j in range(-3, ny + 3)]
        for j, value in enumerate(y_terms(u, [speed_sign(p) for p in paces])):
            emit(x, j, u[j + 3], paces[j], value)

    over_rows(geo, row)


def x_pass(src, pace, faces, geo, emit):
    ny, x_lo, x_hi, _ = geo
    unroll = (x_hi - x_lo) // 4

    def tile(x, j):
        return load_tile(src, geo, x, j)

    def advance(x, j, state):
        d, e, sixth, g, h, pp0, pp1, p2, ql, qr, left = state
        d2 = tile(x + 3, j) - tile(x + 2, j)
        e2 = 0.5 * (d2 - d)
        g2 = e2 - e
        sixth2 = g2 * (1.0 / 6.0)
        pp2, pt2, pm2, half = pair_weights(e, e2, g2)
        ql2, qr2 = central(d, sixth2, half)
        h2 = sixth2 - sixth
        left2, right = face_values(pp0, p2, pm2, h, h2, ql, qr)
        return left, right, (d2, e2, sixth2, g2, h2, pp1, pp2, pt2, ql2, qr2, left2)

    def column(j, carry):
        zero = jnp.zeros((8, NZ), F32)
        x = x_lo - 1
        u = [tile(x + k, j) for k in range(-2, 3)]
        ds = [u[k + 1] - u[k] for k in range(4)]
        es = [0.5 * (ds[k + 1] - ds[k]) for k in range(3)]
        g0, g1 = es[1] - es[0], es[2] - es[1]
        ppa, _, _, _ = pair_weights(es[0], es[1], g0)
        ppb, ptb, _, half = pair_weights(es[1], es[2], g1)
        s0, s1 = g0 * (1.0 / 6.0), g1 * (1.0 / 6.0)
        ql, qr = central(ds[2], s1, half)
        state = (ds[3], es[2], s1, g1, s1 - s0, ppa, ppb, ptb, ql, qr, zero)
        _, _, state = advance(x, j, state)

        def body(i, state):
            for k in range(unroll):
                x = x_lo + i * unroll + k
                left, right, state = advance(x, j, state)
                at = packed(geo, x, j)
                z_left, z_right = prev_z(faces[0][at, :]), faces[1][at, :]
                if pace is None:
                    rising = rise(left, right) + rise(z_left, z_right)
                    falling = fall(left, right) + fall(z_left, z_right)
                    emit(x, j, tile(x, j), rising, falling)
                    continue
                p = load_tile(pace, geo, x, j)
                sign = speed_sign(p)
                total = upwind(sign, left, right) + upwind(sign, z_left, z_right)
                emit(x, j, tile(x, j), p, total)
            return state

        lax.fori_loop(0, 4, body, state)
        return carry

    lax.fori_loop(0, ny, column, 0)


def stage(src, slopes, pace, term, faces, geo, finish):
    def keep(x, j, u, p, value):
        term[packed(geo, x, j), :] = value
        z_row(slopes, faces, geo, x, j)

    def join(x, j, u, p, value):
        finish(x, j, u, u + p * root(value + term[packed(geo, x, j), :]))

    y_pass(src, pace, geo, keep)
    x_pass(src, pace, faces, geo, join)


def fill_block(ext, own, before, after, width, slopes=None):
    def put(src, x_to, count, group):
        def body(n, carry):
            for k in range(group):
                x = n * group + k
                for i in range(CY // 8):
                    value = src[pl.ds(pl.multiple_of(x * CY + 8 * i, 8), 8), :]
                    at = pl.ds(pl.multiple_of((x + x_to) * YP + (YO + 8 * i), 8), 8)
                    ext[at, :] = value
                    if slopes:
                        slopes[0][at, :], slopes[1][at, :] = z_slopes(value)
            return carry

        lax.fori_loop(0, count // group, body, 0)

    put(own, XO, CX, 8)
    put(before, XO - width, width, width)
    put(after, XO + CX, width, width)


def fill_sides(ext, before, after, width, slopes=None):
    for t in range(width):
        for b in range(XR // 8):
            for src, y in ((before, YO - width + t), (after, YO + CY + t)):
                value = src[pl.ds(t * XR + 8 * b, 8), :]
                at = pl.ds(b * 8 * YP + y, 8, stride=YP)
                ext[at, :] = value
                if slopes:
                    slopes[0][at, :], slopes[1][at, :] = z_slopes(value)


def sides_kernel(width, own, before, after, low, high, ext):
    fill_block(ext, own, before, after, width)
    for t in range(width):
        for b in range(XR // 8):
            low[pl.ds(t * XR + 8 * b, 8), :] = ext[pl.ds(b * 8 * YP + (YO + t), 8, stride=YP), :]
            high[pl.ds(t * XR + 8 * b, 8), :] = ext[
                pl.ds(b * 8 * YP + (YO + CY - width + t), 8, stride=YP), :
            ]


def params():
    return pltpu.CompilerParams(vmem_limit_bytes=VMEM_LIMIT)


def shape(rows):
    return jax.ShapeDtypeStruct((rows, NZ), F32)


def vmem(rows):
    return pltpu.VMEM((rows, NZ), F32)


def shift_pair(low, high, axis):
    size = lax.axis_size(axis)
    up = [(i, (i + 1) % size) for i in range(size)]
    down = [(j, i) for i, j in up]
    return lax.ppermute(high, axis, up), lax.ppermute(low, axis, down)


def sides_call(pieces, width):
    return pl.pallas_call(
        functools.partial(sides_kernel, width),
        out_shape=(shape(width * XR), shape(width * XR)),
        scratch_shapes=[vmem(EXT)],
        compiler_params=params(),
        cost_estimate=cost(1),
        name="sides",
    )(*pieces)


def cross_x(own, low, high, width):
    pieces = (own, *shift_pair(low, high, "gx"))
    return pieces, sides_call(pieces, width)


def cost(us):
    return pl.CostEstimate(
        flops=1000 * us, bytes_accessed=int(3.0e6 * us), transcendentals=0
    )


def own_geometry(width):
    _, x_lo, x_hi, _ = geometry(width, width - 3)
    return (CY // 8, x_lo, x_hi, YO)


def early_kernel(width, signed, *refs):
    refs = list(refs)
    own, before, after = refs[:3]
    refs = refs[3:]
    pace = refs.pop(0) if signed else None
    outs = [refs.pop(0) for _ in range(1 if signed else 2)]
    base, slopes, faces = refs[0], refs[1:3], refs[3:5]
    fill_block(base, own, before, after, width, slopes)
    geo = own_geometry(width)

    def row(x):
        for j in range(geo[0]):
            z_row(slopes, faces, geo, x, j)

    over_rows(geo, row)

    def emit(x, j, u, *values):
        for out, value in zip(outs, values[-len(outs) :]):
            out[packed(geo, x, j), :] = value

    x_pass(base, pace, faces, geo, emit)


def early_call(width, pieces, pace=None):
    signed = pace is not None
    return pl.pallas_call(
        functools.partial(early_kernel, width, signed),
        out_shape=(shape(XR * CY),) * (1 if signed else 2),
        scratch_shapes=[vmem(EXT)] * 3 + [vmem(XR * CY)] * 2,
        compiler_params=params(),
        cost_estimate=cost(10),
        name="early",
    )(*pieces, *((pace,) if signed else ()))


def runge_kutta(width, next_width, make_pace, *refs):
    refs = list(refs)
    own, before, after, left, right = refs[:5]
    refs = refs[5:]
    early = [refs.pop(0) for _ in range(2 if make_pace else 1)]
    if make_pace:
        p_own, p_before, p_after, p_left, p_right = refs[:5]
        refs = refs[5:]
    else:
        pace = refs.pop(0)
    out = refs.pop(0)
    if next_width:
        out_low, out_high = refs[:2]
        refs = refs[2:]
    if make_pace:
        pace = refs.pop(0)
    base, first, second = refs[:3]
    even, odd, term, faces = refs[3:5], refs[5:7], refs[7], refs[8:10]

    fill_block(base, own, before, after, width)
    fill_sides(base, left, right, width, even)
    if make_pace:
        fill_block(pace, p_own, p_before, p_after, SPEED_HALO)
        fill_sides(pace, p_left, p_right, SPEED_HALO)

    def finish_one(geo):
        def finish(x, j, u, moved):
            store_tile(first, geo, x, j, moved)
            store_slopes(odd, geo, x, j, moved)

        return finish

    inner = own_geometry(width)
    done = finish_one(inner)

    def join(x, j, u, p, value):
        at = packed(inner, x, j)
        if make_pace:
            value += jnp.where(p <= 0.0, early[0][at, :], early[1][at, :])
        else:
            value += early[0][at, :]
        done(x, j, u, u + p * root(value))

    y_pass(base, pace, inner, join)
    for y_lo in (YO - 8, YO + CY):
        side = (1, inner[1], inner[2], y_lo)
        stage(base, even, pace, term, faces, side, finish_one(side))

    geo2 = geometry(width, width - 6)

    def finish_two(x, j, u, moved):
        value = 0.75 * load_tile(base, geo2, x, j) + 0.25 * moved
        store_tile(second, geo2, x, j, value)
        store_slopes(even, geo2, x, j, value)

    stage(first, odd, pace, term, faces, geo2, finish_two)

    geo3 = geometry(width, width - 9)

    def finish_three(x, j, u, moved):
        value = (1.0 / 3.0) * load_tile(base, geo3, x, j) + (2.0 / 3.0) * moved
        if next_width:
            out[pl.ds((x - XO) * CY + j, 8, stride=geo3[0]), :] = value
        else:
            store_tile(first, geo3, x, j, value)

    stage(second, even, pace, term, faces, geo3, finish_three)

    if next_width:
        rows = next_width * CY
        out_low[...] = out[pl.ds(0, rows), :]
        out_high[...] = out[pl.ds(COLS - rows, rows), :]
        return

    def sweep(src, geo, store):
        ny = geo[0]

        def row(x):
            u = [load_tile(src, geo, x, j) for j in range(-1, ny + 1)]
            for j in range(ny):
                v = u[j + 1]
                advected = load_tile(first, geo, x, j)
                sign = sign_of(advected)
                total = upwind(sign, v - u[j], v - u[j + 2])
                total += upwind(
                    sign,
                    v - load_tile(src, geo, x - 1, j),
                    v - load_tile(src, geo, x + 1, j),
                )
                total += upwind(sign, v - prev_z(v), v - next_z(v))
                smooth = advected * lax.rsqrt(advected * advected + 1.0)
                store(x, j, v - PSEUDO_STEP * smooth * (root(total) - 1.0))

        over_rows(geo, row)

    wide, block = geometry(width, 1), geometry(width, 0)
    sweep(first, wide, lambda x, j, v: store_tile(second, wide, x, j, v))

    def store_out(x, j, v):
        out[pl.ds((x - XO) * CY + j, 8, stride=block[0]), :] = v

    sweep(second, block, store_out)


def step_call(width, next_width, pieces, early, pace):
    make_pace = isinstance(pace, tuple)
    outs = [shape(COLS)]
    if next_width:
        outs += [shape(next_width * CY)] * 2
    if make_pace:
        outs += [shape(EXT)]
    return pl.pallas_call(
        functools.partial(runge_kutta, width, next_width, make_pace),
        out_shape=tuple(outs),
        scratch_shapes=[vmem(EXT)] * 7 + [vmem(XR * 56)] * 3,
        compiler_params=params(),
        cost_estimate=cost(35),
        name="step",
    )(*pieces, *early, *(pace if make_pace else (pace,)))


def split(x):
    high = x.astype(jnp.bfloat16)
    low = (x - high.astype(F32)).astype(jnp.bfloat16)
    return jnp.concatenate([high, low], axis=1)


def onehot(mask):
    return jnp.where(mask, 1.0, 0.0).astype(jnp.bfloat16)


def pack_kernel(rows, owner, column, send, parts):
    count = rows.shape[0]
    own = owner[...]
    tags = onehot(lax.broadcasted_iota(jnp.int32, (DEVICES, count), 0) == own)
    order = onehot(
        lax.broadcasted_iota(jnp.int32, (count, count), 0)
        < lax.broadcasted_iota(jnp.int32, (count, count), 1)
    )
    earlier = jnp.dot(tags, order, preferred_element_type=F32)
    rank = jnp.sum(earlier * tags.astype(F32), axis=0, keepdims=True).astype(jnp.int32)
    target = own * SLOTS + rank
    parts[...] = split(rows[...])

    block = 128

    def body(b, carry):
        slot = lax.broadcasted_iota(jnp.int32, (block, count), 0) + b * block
        both = jnp.dot(onehot(slot == target), parts[...], preferred_element_type=F32)
        send[pl.ds(pl.multiple_of(b * block, block), block), :] = both[:, :NZ] + both[:, NZ:]
        return carry

    lax.fori_loop(0, DEVICES * SLOTS // block, body, 0)

    place = lax.broadcasted_iota(jnp.int32, (NZ, count), 0) == rank
    number = column[...] + 1
    dims = (((1,), (1,)), ((), ()))
    total = jnp.zeros((DEVICES, NZ), F32)
    for part, scale in ((number >> 6, 64.0), (number & 63, 1.0)):
        held = jnp.where(place, part.astype(F32), 0.0).astype(jnp.bfloat16)
        total += scale * lax.dot_general(tags, held, dims, preferred_element_type=F32)
    for b in range(DEVICES // 8):
        send[pl.ds(b * 8 * SLOTS + CAP, 8, stride=SLOTS), :] = total[8 * b : 8 * b + 8]


def unpack_kernel(low_rows, got, mask, speed, speed_low, speed_high, parts, number):
    for b in range(DEVICES // 8):
        number[pl.ds(8 * b, 8), :] = got[pl.ds(b * 8 * SLOTS + CAP, 8, stride=SLOTS), :]
    columns = number[...].T.astype(jnp.int32) - 1
    for k in range(CAP):
        for b in range(DEVICES // 16):
            pair = [
                got[pl.ds((b * 16 + 8 * i) * SLOTS + k, 8, stride=SLOTS), :] for i in range(2)
            ]
            parts[pl.ds(k * DEVICES + 16 * b, 16), :] = split(jnp.concatenate(pair, axis=0))
    named = jnp.concatenate([columns[k : k + 1, :] for k in range(CAP)], axis=1)

    block = 128

    def body(b, carry):
        cell = lax.broadcasted_iota(jnp.int32, (block, CAP * DEVICES), 0) + b * block
        both = jnp.dot(onehot(cell == named), parts[...], preferred_element_type=F32)
        at = pl.ds(pl.multiple_of(b * block, block), block)
        speed[at, :] = (both[:, :NZ] + both[:, NZ:]) * (mask[at, :] * -TIME_STEP)
        return carry

    lax.fori_loop(0, COLS // block, body, 0)
    speed_low[...] = speed[pl.ds(0, low_rows), :]
    speed_high[...] = speed[pl.ds(COLS - low_rows, low_rows), :]


def shards(level_set, band_mask, rows, row_owner, row_tile):
    count = rows.shape[0]
    send = pl.pallas_call(
        pack_kernel,
        out_shape=shape(DEVICES * SLOTS),
        scratch_shapes=[pltpu.VMEM((count, 2 * NZ), jnp.bfloat16)],
        compiler_params=params(),
        cost_estimate=cost(5),
        name="pack",
    )(rows, row_owner.reshape(1, count), row_tile.reshape(1, count))
    u = level_set.reshape(COLS, NZ)
    before, after = shift_pair(u[: 9 * CY], u[COLS - 9 * CY :], "gx")
    send, before, after = lax.optimization_barrier((send, before, after))
    got = lax.all_to_all(
        send.reshape(DEVICES, 1, SLOTS * NZ), ("gx", "gy"), split_axis=0, concat_axis=0, tiled=True
    ).reshape(DEVICES * SLOTS, NZ)
    pieces = (u, before, after)
    sides = sides_call(pieces, 9)
    early = early_call(9, pieces)
    pieces = (*pieces, *shift_pair(*sides, "gy"))
    got, early = lax.optimization_barrier((got, early))

    mask = band_mask.astype(F32).reshape(COLS, 1)
    face = SPEED_HALO * CY
    pace, pace_low, pace_high = pl.pallas_call(
        functools.partial(unpack_kernel, face),
        out_shape=(shape(COLS), shape(face), shape(face)),
        scratch_shapes=[pltpu.VMEM((CAP * DEVICES, 2 * NZ), jnp.bfloat16), vmem(DEVICES)],
        compiler_params=params(),
        name="unpack",
    )(got, mask)
    pace_low, pace_high, pieces = lax.optimization_barrier((pace_low, pace_high, pieces))
    paces, sides = cross_x(pace, pace_low, pace_high, SPEED_HALO)
    paces = (*paces, *shift_pair(*sides, "gy"))
    u, low, high, pace = step_call(9, 9, pieces, early, paces)

    for width, next_width in ((9, 11), (11, 0)):
        pieces, sides = cross_x(u, low, high, width)
        early = early_call(width, pieces, pace)
        pieces = (*pieces, *shift_pair(*sides, "gy"))
        u, *faces = step_call(width, next_width, pieces, early, pace)
        low, high = faces or (None, None)
    return u.reshape(CX, CY, NZ)


def solution(mesh):
    return jax.shard_map(
        shards,
        mesh=mesh,
        in_specs=(
            P("gx", "gy", None),
            P("gx", "gy"),
            P(("gx", "gy"), None),
            P(("gx", "gy"), None),
            P(("gx", "gy")),
        ),
        out_specs=P("gx", "gy", None),
        check_vma=False,
    )
```

```python
import functools

import jax
import jax.numpy as jnp
from jax import lax
from jax.experimental import pallas as pl
from jax.experimental.pallas import tpu as pltpu
from jax.sharding import PartitionSpec as P

EPSILON = 1e-06
TIME_STEP = 0.2
PSEUDO_STEP = 0.3

CX, CY, NZ = 64, 40, 128
DEVICES = 128
CAP = 16
SLOTS = CAP + 1
COLS = CX * CY

XO, YO = 12, 16
XR, YP = 88, 72
EXT = XR * YP
SPEED_HALO = 8
VMEM_LIMIT = 40 * 1024 * 1024
F32 = jnp.float32


def rcp(x):
    return pl.reciprocal(x, approx=True)


QUARTER = 0.25 * EPSILON


def pair_weights(e_left, e_right, g):
    total = e_left + e_right
    half = 0.5 * total
    square = g * g
    centre = half * half + (square * (13.0 / 12.0) + QUARTER)
    ends = centre + square
    cross = total * g
    ip = rcp(ends + cross)
    it = rcp(centre)
    im = rcp(ends - cross)
    return ip * ip, it * it * 3.0, im * im, half


def weight_end(half, g):
    i = rcp(half * half + (g * g * (13.0 / 12.0) + QUARTER))
    return i * i


def central(slope, sixth, half):
    base = slope + sixth
    return base + half, half - base


def face_values(p1, p2, p3, h_left, h_right, q_left, q_right):
    low = p1 * h_left
    high = p3 * h_right
    both = 0.5 * (p1 + p3) + p2
    twice = low + high
    twice = twice + twice
    left = q_left - (twice + high) * rcp(both + p3)
    right = q_right - (twice + low) * rcp(both + p1)
    return left, right


def upwind(sign, left, right):
    top = jnp.maximum(jnp.maximum(sign * left, sign * right), 0.0)
    return top * top


def rise(left, right):
    top = jnp.maximum(jnp.maximum(left, right), 0.0)
    return top * top


def fall(left, right):
    top = jnp.minimum(jnp.minimum(left, right), 0.0)
    return top * top


def sign_of(value):
    return jnp.where(value >= 0.0, 1.0, -1.0)


def speed_sign(pace):
    return jnp.where(pace <= 0.0, 1.0, -1.0)


def root(x):
    return x * lax.rsqrt(jnp.maximum(x, 1e-37))


def prev_z(x):
    return pltpu.roll(x, 1, 1)


def next_z(x):
    return pltpu.roll(x, NZ - 1, 1)


def z_slopes(u):
    after = next_z(u)
    return after - u, 0.5 * (after + prev_z(u)) - u


def z_faces(d, e):
    e_prev, e_next, e_after = prev_z(e), next_z(e), pltpu.roll(e, NZ - 2, 1)
    g_prev, g, g_next = e - e_prev, e_next - e, e_after - e_next
    sixth = g * (1.0 / 6.0)
    h = sixth - g_prev * (1.0 / 6.0)
    h_next = g_next * (1.0 / 6.0) - sixth
    half = 0.5 * (e + e_next)
    pp = weight_end(0.5 * (e_prev + e) + g_prev, g_prev)
    pt = weight_end(half, g) * 3.0
    pm = weight_end(0.5 * (e_next + e_after) - g_next, g_next)
    return face_values(pp, pt, pm, h, h_next, *central(d, sixth, half))


def y_terms(u, signs):
    n = len(u) - 6
    out = []
    d, e, sixth, h, pp, pt, pm, q, left = {}, {}, {}, {}, {}, {}, {}, {}, {}
    d[0] = u[1] - u[0]
    for k in range(1, n + 5):
        d[k] = u[k + 1] - u[k]
        e[k] = 0.5 * (d[k] - d[k - 1])
        if k >= 2:
            f = k - 1
            g = e[k] - e[f]
            sixth[f] = g * (1.0 / 6.0)
            pp[f], pt[f], pm[f], half = pair_weights(e[f], e[k], g)
            q[f] = central(d[f], sixth[f], half)
            if f >= 2:
                h[f] = sixth[f] - sixth[f - 1]
            if f >= 3:
                w = f - 1
                lw, rw = face_values(pp[w - 1], pt[w], pm[w + 1], h[w], h[w + 1], *q[w])
                left[w] = lw
                if w >= 3:
                    out.append(upwind(signs[w - 3], left[w - 1], rw))
    return out


GROUP = 4
ROW_GROUP = 4
SIDE_TURNS = 2
TURNS = 2


def geometry(width, margin):
    count = (CX + 2 * margin + GROUP - 1) // GROUP * GROUP
    return ((CY + 2 * margin + 7) // 8, XO - margin, XO - margin + count, YO - margin)


def load_tile(ref, geo, x, j):
    return ref[pl.ds(x * YP + (geo[3] + j), 8, stride=geo[0]), :]


def store_tile(ref, geo, x, j, value):
    ref[pl.ds(x * YP + (geo[3] + j), 8, stride=geo[0]), :] = value


def store_slopes(slopes, geo, x, j, value):
    d, e = z_slopes(value)
    store_tile(slopes[0], geo, x, j, d)
    store_tile(slopes[1], geo, x, j, e)


def packed(geo, x, j):
    return pl.ds(pl.multiple_of(x * (8 * geo[0]) + 8 * j, 8), 8)


def over_rows(geo, row):
    group = (geo[2] - geo[1]) // SIDE_TURNS if geo[0] == 1 else ROW_GROUP

    def body(i, carry):
        for k in range(group):
            row(geo[1] + i * group + k)
        return carry

    lax.fori_loop(0, (geo[2] - geo[1]) // group, body, 0)


def z_row(slopes, faces, geo, x, j):
    left, right = z_faces(load_tile(slopes[0], geo, x, j), load_tile(slopes[1], geo, x, j))
    faces[0][packed(geo, x, j), :] = left
    faces[1][packed(geo, x, j), :] = right


def y_pass(src, pace, geo, emit):
    ny = geo[0]

    def row(x):
        paces = [load_tile(pace, geo, x, j) for j in range(ny)]
        u = [load_tile(src, geo, x, j) for j in range(-3, ny + 3)]
        for j, value in enumerate(y_terms(u, [speed_sign(p) for p in paces])):
            emit(x, j, u[j + 3], paces[j], value)

    over_rows(geo, row)


def x_pass(src, pace, faces, geo, emit):
    ny, x_lo, x_hi, _ = geo
    unroll = (x_hi - x_lo) // TURNS

    def tile(x, j):
        return load_tile(src, geo, x, j)

    def advance(x, j, state):
        d, e, sixth, g, h, pp0, pp1, p2, ql, qr, left = state
        d2 = tile(x + 3, j) - tile(x + 2, j)
        e2 = 0.5 * (d2 - d)
        g2 = e2 - e
        sixth2 = g2 * (1.0 / 6.0)
        pp2, pt2, pm2, half = pair_weights(e, e2, g2)
        ql2, qr2 = central(d, sixth2, half)
        h2 = sixth2 - sixth
        left2, right = face_values(pp0, p2, pm2, h, h2, ql, qr)
        return left, right, (d2, e2, sixth2, g2, h2, pp1, pp2, pt2, ql2, qr2, left2)

    def column(j, carry):
        zero = jnp.zeros((8, NZ), F32)
        x = x_lo - 1
        u = [tile(x + k, j) for k in range(-2, 3)]
        ds = [u[k + 1] - u[k] for k in range(4)]
        es = [0.5 * (ds[k + 1] - ds[k]) for k in range(3)]
        g0, g1 = es[1] - es[0], es[2] - es[1]
        ppa, _, _, _ = pair_weights(es[0], es[1], g0)
        ppb, ptb, _, half = pair_weights(es[1], es[2], g1)
        s0, s1 = g0 * (1.0 / 6.0), g1 * (1.0 / 6.0)
        ql, qr = central(ds[2], s1, half)
        state = (ds[3], es[2], s1, g1, s1 - s0, ppa, ppb, ptb, ql, qr, zero)
        _, _, state = advance(x, j, state)

        def body(i, state):
            for k in range(unroll):
                x = x_lo + i * unroll + k
                left, right, state = advance(x, j, state)
                at = packed(geo, x, j)
                z_left, z_right = prev_z(faces[0][at, :]), faces[1][at, :]
                if pace is None:
                    rising = rise(left, right) + rise(z_left, z_right)
                    falling = fall(left, right) + fall(z_left, z_right)
                    emit(x, j, tile(x, j), rising, falling)
                    continue
                p = load_tile(pace, geo, x, j)
                sign = speed_sign(p)
                total = upwind(sign, left, right) + upwind(sign, z_left, z_right)
                emit(x, j, tile(x, j), p, total)
            return state

        lax.fori_loop(0, TURNS, body, state)
        return carry

    lax.fori_loop(0, ny, column, 0)


def stage(src, slopes, pace, term, faces, geo, finish):
    def keep(x, j, u, p, value):
        term[packed(geo, x, j), :] = value
        z_row(slopes, faces, geo, x, j)

    def join(x, j, u, p, value):
        finish(x, j, u, u + p * root(value + term[packed(geo, x, j), :]))

    y_pass(src, pace, geo, keep)
    x_pass(src, pace, faces, geo, join)


def fill_block(ext, own, before, after, width, slopes=None):
    def put(src, x_to, count, group):
        def body(n, carry):
            for k in range(group):
                x = n * group + k
                for i in range(CY // 8):
                    value = src[pl.ds(pl.multiple_of(x * CY + 8 * i, 8), 8), :]
                    at = pl.ds(pl.multiple_of((x + x_to) * YP + (YO + 8 * i), 8), 8)
                    ext[at, :] = value
                    if slopes:
                        slopes[0][at, :], slopes[1][at, :] = z_slopes(value)
            return carry

        lax.fori_loop(0, count // group, body, 0)

    put(own, XO, CX, 8)
    put(before, XO - width, width, width)
    put(after, XO + CX, width, width)


def fill_sides(ext, before, after, width, slopes=None):
    for t in range(width):
        for b in range(XR // 8):
            for src, y in ((before, YO - width + t), (after, YO + CY + t)):
                value = src[pl.ds(t * XR + 8 * b, 8), :]
                at = pl.ds(b * 8 * YP + y, 8, stride=YP)
                ext[at, :] = value
                if slopes:
                    slopes[0][at, :], slopes[1][at, :] = z_slopes(value)


def sides_kernel(width, own, before, after, low, high, ext):
    fill_block(ext, own, before, after, width)
    for t in range(width):
        for b in range(XR // 8):
            low[pl.ds(t * XR + 8 * b, 8), :] = ext[pl.ds(b * 8 * YP + (YO + t), 8, stride=YP), :]
            high[pl.ds(t * XR + 8 * b, 8), :] = ext[
                pl.ds(b * 8 * YP + (YO + CY - width + t), 8, stride=YP), :
            ]


def params():
    return pltpu.CompilerParams(vmem_limit_bytes=VMEM_LIMIT)


def shape(rows):
    return jax.ShapeDtypeStruct((rows, NZ), F32)


def vmem(rows):
    return pltpu.VMEM((rows, NZ), F32)


def shift_pair(low, high, axis):
    size = lax.axis_size(axis)
    up = [(i, (i + 1) % size) for i in range(size)]
    down = [(j, i) for i, j in up]
    return lax.ppermute(high, axis, up), lax.ppermute(low, axis, down)


def sides_call(pieces, width):
    return pl.pallas_call(
        functools.partial(sides_kernel, width),
        out_shape=(shape(width * XR), shape(width * XR)),
        scratch_shapes=[vmem(EXT)],
        compiler_params=params(),
        cost_estimate=cost(1),
        name="sides",
    )(*pieces)


def cross_x(own, low, high, width):
    pieces = (own, *shift_pair(low, high, "gx"))
    return pieces, sides_call(pieces, width)


def cost(us):
    return pl.CostEstimate(
        flops=1000 * us, bytes_accessed=int(3.0e6 * us), transcendentals=0
    )


def own_geometry(width):
    _, x_lo, x_hi, _ = geometry(width, width - 3)
    return (CY // 8, x_lo, x_hi, YO)


def early_kernel(width, signed, *refs):
    refs = list(refs)
    own, before, after = refs[:3]
    refs = refs[3:]
    pace = refs.pop(0) if signed else None
    outs = [refs.pop(0) for _ in range(1 if signed else 2)]
    base, slopes, faces = refs[0], refs[1:3], refs[3:5]
    fill_block(base, own, before, after, width, slopes)
    geo = own_geometry(width)

    def row(x):
        for j in range(geo[0]):
            z_row(slopes, faces, geo, x, j)

    over_rows(geo, row)

    def emit(x, j, u, *values):
        for out, value in zip(outs, values[-len(outs) :]):
            out[packed(geo, x, j), :] = value

    x_pass(base, pace, faces, geo, emit)


def early_call(width, pieces, pace=None):
    signed = pace is not None
    return pl.pallas_call(
        functools.partial(early_kernel, width, signed),
        out_shape=(shape(XR * CY),) * (1 if signed else 2),
        scratch_shapes=[vmem(EXT)] * 3 + [vmem(XR * CY)] * 2,
        compiler_params=params(),
        cost_estimate=cost(10),
        name="early",
    )(*pieces, *((pace,) if signed else ()))


def runge_kutta(width, next_width, make_pace, *refs):
    refs = list(refs)
    own, before, after, left, right = refs[:5]
    refs = refs[5:]
    early = [refs.pop(0) for _ in range(2 if make_pace else 1)]
    if make_pace:
        p_own, p_before, p_after, p_left, p_right = refs[:5]
        refs = refs[5:]
    else:
        pace = refs.pop(0)
    out = refs.pop(0)
    if next_width:
        out_low, out_high = refs[:2]
        refs = refs[2:]
    if make_pace:
        pace = refs.pop(0)
    base, first, second = refs[:3]
    even, odd, term, faces = refs[3:5], refs[5:7], refs[7], refs[8:10]

    fill_block(base, own, before, after, width)
    fill_sides(base, left, right, width, even)
    if make_pace:
        fill_block(pace, p_own, p_before, p_after, SPEED_HALO)
        fill_sides(pace, p_left, p_right, SPEED_HALO)

    def finish_one(geo):
        def finish(x, j, u, moved):
            store_tile(first, geo, x, j, moved)
            store_slopes(odd, geo, x, j, moved)

        return finish

    inner = own_geometry(width)
    done = finish_one(inner)

    def join(x, j, u, p, value):
        at = packed(inner, x, j)
        if make_pace:
            value += jnp.where(p <= 0.0, early[0][at, :], early[1][at, :])
        else:
            value += early[0][at, :]
        done(x, j, u, u + p * root(value))

    y_pass(base, pace, inner, join)
    for y_lo in (YO - 8, YO + CY):
        side = (1, inner[1], inner[2], y_lo)
        stage(base, even, pace, term, faces, side, finish_one(side))

    geo2 = geometry(width, width - 6)

    def finish_two(x, j, u, moved):
        value = 0.75 * load_tile(base, geo2, x, j) + 0.25 * moved
        store_tile(second, geo2, x, j, value)
        store_slopes(even, geo2, x, j, value)

    stage(first, odd, pace, term, faces, geo2, finish_two)

    geo3 = geometry(width, width - 9)

    def finish_three(x, j, u, moved):
        value = (1.0 / 3.0) * load_tile(base, geo3, x, j) + (2.0 / 3.0) * moved
        if next_width:
            out[pl.ds((x - XO) * CY + j, 8, stride=geo3[0]), :] = value
        else:
            store_tile(first, geo3, x, j, value)

    stage(second, even, pace, term, faces, geo3, finish_three)

    if next_width:
        rows = next_width * CY
        out_low[...] = out[pl.ds(0, rows), :]
        out_high[...] = out[pl.ds(COLS - rows, rows), :]
        return

    def sweep(src, geo, store):
        ny = geo[0]

        def row(x):
            u = [load_tile(src, geo, x, j) for j in range(-1, ny + 1)]
            for j in range(ny):
                v = u[j + 1]
                advected = load_tile(first, geo, x, j)
                sign = sign_of(advected)
                total = upwind(sign, v - u[j], v - u[j + 2])
                total += upwind(
                    sign,
                    v - load_tile(src, geo, x - 1, j),
                    v - load_tile(src, geo, x + 1, j),
                )
                total += upwind(sign, v - prev_z(v), v - next_z(v))
                smooth = advected * lax.rsqrt(advected * advected + 1.0)
                store(x, j, v - PSEUDO_STEP * smooth * (root(total) - 1.0))

        over_rows(geo, row)

    wide, block = geometry(width, 1), geometry(width, 0)
    sweep(first, wide, lambda x, j, v: store_tile(second, wide, x, j, v))

    def store_out(x, j, v):
        out[pl.ds((x - XO) * CY + j, 8, stride=block[0]), :] = v

    sweep(second, block, store_out)


def step_call(width, next_width, pieces, early, pace):
    make_pace = isinstance(pace, tuple)
    outs = [shape(COLS)]
    if next_width:
        outs += [shape(next_width * CY)] * 2
    if make_pace:
        outs += [shape(EXT)]
    return pl.pallas_call(
        functools.partial(runge_kutta, width, next_width, make_pace),
        out_shape=tuple(outs),
        scratch_shapes=[vmem(EXT)] * 7 + [vmem(XR * 56)] * 3,
        compiler_params=params(),
        cost_estimate=cost(35),
        name="step",
    )(*pieces, *early, *(pace if make_pace else (pace,)))


def split(x):
    high = x.astype(jnp.bfloat16)
    low = (x - high.astype(F32)).astype(jnp.bfloat16)
    return jnp.concatenate([high, low], axis=1)


def onehot(mask):
    return jnp.where(mask, 1.0, 0.0).astype(jnp.bfloat16)


def pack_kernel(rows, owner, column, send, parts):
    count = rows.shape[0]
    own = owner[...]
    tags = onehot(lax.broadcasted_iota(jnp.int32, (DEVICES, count), 0) == own)
    order = onehot(
        lax.broadcasted_iota(jnp.int32, (count, count), 0)
        < lax.broadcasted_iota(jnp.int32, (count, count), 1)
    )
    earlier = jnp.dot(tags, order, preferred_element_type=F32)
    rank = jnp.sum(earlier * tags.astype(F32), axis=0, keepdims=True).astype(jnp.int32)
    target = own * SLOTS + rank
    parts[...] = split(rows[...])

    block = 128

    def body(b, carry):
        slot = lax.broadcasted_iota(jnp.int32, (block, count), 0) + b * block
        both = jnp.dot(onehot(slot == target), parts[...], preferred_element_type=F32)
        send[pl.ds(pl.multiple_of(b * block, block), block), :] = both[:, :NZ] + both[:, NZ:]
        return carry

    lax.fori_loop(0, DEVICES * SLOTS // block, body, 0)

    place = lax.broadcasted_iota(jnp.int32, (NZ, count), 0) == rank
    number = column[...] + 1
    dims = (((1,), (1,)), ((), ()))
    total = jnp.zeros((DEVICES, NZ), F32)
    for part, scale in ((number >> 6, 64.0), (number & 63, 1.0)):
        held = jnp.where(place, part.astype(F32), 0.0).astype(jnp.bfloat16)
        total += scale * lax.dot_general(tags, held, dims, preferred_element_type=F32)
    for b in range(DEVICES // 8):
        send[pl.ds(b * 8 * SLOTS + CAP, 8, stride=SLOTS), :] = total[8 * b : 8 * b + 8]


def unpack_kernel(low_rows, got, mask, speed, speed_low, speed_high, parts, number):
    for b in range(DEVICES // 8):
        number[pl.ds(8 * b, 8), :] = got[pl.ds(b * 8 * SLOTS + CAP, 8, stride=SLOTS), :]
    columns = number[...].T.astype(jnp.int32) - 1
    for k in range(CAP):
        for b in range(DEVICES // 16):
            pair = [
                got[pl.ds((b * 16 + 8 * i) * SLOTS + k, 8, stride=SLOTS), :] for i in range(2)
            ]
            parts[pl.ds(k * DEVICES + 16 * b, 16), :] = split(jnp.concatenate(pair, axis=0))
    named = jnp.concatenate([columns[k : k + 1, :] for k in range(CAP)], axis=1)

    block = 128

    def body(b, carry):
        cell = lax.broadcasted_iota(jnp.int32, (block, CAP * DEVICES), 0) + b * block
        both = jnp.dot(onehot(cell == named), parts[...], preferred_element_type=F32)
        at = pl.ds(pl.multiple_of(b * block, block), block)
        speed[at, :] = (both[:, :NZ] + both[:, NZ:]) * (mask[at, :] * -TIME_STEP)
        return carry

    lax.fori_loop(0, COLS // block, body, 0)
    speed_low[...] = speed[pl.ds(0, low_rows), :]
    speed_high[...] = speed[pl.ds(COLS - low_rows, low_rows), :]


def shards(level_set, band_mask, rows, row_owner, row_tile):
    count = rows.shape[0]
    send = pl.pallas_call(
        pack_kernel,
        out_shape=shape(DEVICES * SLOTS),
        scratch_shapes=[pltpu.VMEM((count, 2 * NZ), jnp.bfloat16)],
        compiler_params=params(),
        cost_estimate=cost(5),
        name="pack",
    )(rows, row_owner.reshape(1, count), row_tile.reshape(1, count))
    u = level_set.reshape(COLS, NZ)
    before, after = shift_pair(u[: 9 * CY], u[COLS - 9 * CY :], "gx")
    send, before, after = lax.optimization_barrier((send, before, after))
    got = lax.all_to_all(
        send.reshape(DEVICES, 1, SLOTS * NZ), ("gx", "gy"), split_axis=0, concat_axis=0, tiled=True
    ).reshape(DEVICES * SLOTS, NZ)
    pieces = (u, before, after)
    sides = sides_call(pieces, 9)
    early = early_call(9, pieces)
    pieces = (*pieces, *shift_pair(*sides, "gy"))
    got, early = lax.optimization_barrier((got, early))

    mask = band_mask.astype(F32).reshape(COLS, 1)
    face = SPEED_HALO * CY
    pace, pace_low, pace_high = pl.pallas_call(
        functools.partial(unpack_kernel, face),
        out_shape=(shape(COLS), shape(face), shape(face)),
        scratch_shapes=[pltpu.VMEM((CAP * DEVICES, 2 * NZ), jnp.bfloat16), vmem(DEVICES)],
        compiler_params=params(),
        name="unpack",
    )(got, mask)
    pace_low, pace_high, pieces = lax.optimization_barrier((pace_low, pace_high, pieces))
    paces, sides = cross_x(pace, pace_low, pace_high, SPEED_HALO)
    paces = (*paces, *shift_pair(*sides, "gy"))
    u, low, high, pace = step_call(9, 9, pieces, early, paces)

    for width, next_width in ((9, 11), (11, 0)):
        pieces, sides = cross_x(u, low, high, width)
        early = early_call(width, pieces, pace)
        pieces = (*pieces, *shift_pair(*sides, "gy"))
        u, *faces = step_call(width, next_width, pieces, early, pace)
        low, high = faces or (None, None)
    return u.reshape(CX, CY, NZ)


def solution(mesh):
    return jax.shard_map(
        shards,
        mesh=mesh,
        in_specs=(
            P("gx", "gy", None),
            P("gx", "gy"),
            P(("gx", "gy"), None),
            P(("gx", "gy"), None),
            P(("gx", "gy")),
        ),
        out_specs=P("gx", "gy", None),
        check_vma=False,
    )
```

```python
import functools

import jax
import jax.numpy as jnp
from jax import lax
from jax.experimental import pallas as pl
from jax.experimental.pallas import tpu as pltpu
from jax.sharding import PartitionSpec as P

EPSILON = 1e-06
TIME_STEP = 0.2
PSEUDO_STEP = 0.3

CX, CY, NZ = 64, 40, 128
DEVICES = 128
CAP = 16
SLOTS = CAP + 1
COLS = CX * CY

XO, YO = 12, 16
XR, YP = 88, 72
EXT = XR * YP
SPEED_HALO = 8
VMEM_LIMIT = 40 * 1024 * 1024
F32 = jnp.float32


def rcp(x):
    return pl.reciprocal(x, approx=True)


QUARTER = 0.25 * EPSILON


def pair_weights(e_left, e_right, g):
    total = e_left + e_right
    half = 0.5 * total
    square = g * g
    centre = half * half + (square * (13.0 / 12.0) + QUARTER)
    ends = centre + square
    cross = total * g
    ip = rcp(ends + cross)
    it = rcp(centre)
    im = rcp(ends - cross)
    return ip * ip, it * it * 3.0, im * im, half


def weight_end(half, g):
    i = rcp(half * half + (g * g * (13.0 / 12.0) + QUARTER))
    return i * i


def central(slope, sixth, half):
    base = slope + sixth
    return base + half, half - base


def face_values(p1, p2, p3, h_left, h_right, q_left, q_right):
    low = p1 * h_left
    high = p3 * h_right
    both = 0.5 * (p1 + p3) + p2
    twice = low + high
    twice = twice + twice
    left = q_left - (twice + high) * rcp(both + p3)
    right = q_right - (twice + low) * rcp(both + p1)
    return left, right


def upwind(sign, left, right):
    top = jnp.maximum(jnp.maximum(sign * left, sign * right), 0.0)
    return top * top


def rise(left, right):
    top = jnp.maximum(jnp.maximum(left, right), 0.0)
    return top * top


def fall(left, right):
    top = jnp.minimum(jnp.minimum(left, right), 0.0)
    return top * top


def sign_of(value):
    return jnp.where(value >= 0.0, 1.0, -1.0)


def speed_sign(pace):
    return jnp.where(pace <= 0.0, 1.0, -1.0)


def root(x):
    return x * lax.rsqrt(jnp.maximum(x, 1e-37))


def prev_z(x):
    return pltpu.roll(x, 1, 1)


def next_z(x):
    return pltpu.roll(x, NZ - 1, 1)


def z_slopes(u):
    after = next_z(u)
    return after - u, 0.5 * (after + prev_z(u)) - u


def z_faces(d, e):
    e_prev, e_next, e_after = prev_z(e), next_z(e), pltpu.roll(e, NZ - 2, 1)
    g_prev, g, g_next = e - e_prev, e_next - e, e_after - e_next
    sixth = g * (1.0 / 6.0)
    h = sixth - g_prev * (1.0 / 6.0)
    h_next = g_next * (1.0 / 6.0) - sixth
    half = 0.5 * (e + e_next)
    pp = weight_end(0.5 * (e_prev + e) + g_prev, g_prev)
    pt = weight_end(half, g) * 3.0
    pm = weight_end(0.5 * (e_next + e_after) - g_next, g_next)
    return face_values(pp, pt, pm, h, h_next, *central(d, sixth, half))


def y_terms(u, signs):
    n = len(u) - 6
    out = []
    d, e, sixth, h, pp, pt, pm, q, left = {}, {}, {}, {}, {}, {}, {}, {}, {}
    d[0] = u[1] - u[0]
    for k in range(1, n + 5):
        d[k] = u[k + 1] - u[k]
        e[k] = 0.5 * (d[k] - d[k - 1])
        if k >= 2:
            f = k - 1
            g = e[k] - e[f]
            sixth[f] = g * (1.0 / 6.0)
            pp[f], pt[f], pm[f], half = pair_weights(e[f], e[k], g)
            q[f] = central(d[f], sixth[f], half)
            if f >= 2:
                h[f] = sixth[f] - sixth[f - 1]
            if f >= 3:
                w = f - 1
                lw, rw = face_values(pp[w - 1], pt[w], pm[w + 1], h[w], h[w + 1], *q[w])
                left[w] = lw
                if w >= 3:
                    out.append(upwind(signs[w - 3], left[w - 1], rw))
    return out


GROUP = 4
ROW_GROUP = 4
SIDE_TURNS = 2
TURNS = 2


def geometry(width, margin):
    count = (CX + 2 * margin + GROUP - 1) // GROUP * GROUP
    return ((CY + 2 * margin + 7) // 8, XO - margin, XO - margin + count, YO - margin)


def load_tile(ref, geo, x, j):
    return ref[pl.ds(x * YP + (geo[3] + j), 8, stride=geo[0]), :]


def store_tile(ref, geo, x, j, value):
    ref[pl.ds(x * YP + (geo[3] + j), 8, stride=geo[0]), :] = value


def store_slopes(slopes, geo, x, j, value):
    d, e = z_slopes(value)
    store_tile(slopes[0], geo, x, j, d)
    store_tile(slopes[1], geo, x, j, e)


def packed(geo, x, j):
    return pl.ds(pl.multiple_of(x * (8 * geo[0]) + 8 * j, 8), 8)


def over_rows(geo, row):
    group = (geo[2] - geo[1]) // SIDE_TURNS if geo[0] == 1 else ROW_GROUP

    def body(i, carry):
        for k in range(group):
            row(geo[1] + i * group + k)
        return carry

    lax.fori_loop(0, (geo[2] - geo[1]) // group, body, 0)


def z_row(slopes, faces, geo, x, j):
    left, right = z_faces(load_tile(slopes[0], geo, x, j), load_tile(slopes[1], geo, x, j))
    faces[0][packed(geo, x, j), :] = left
    faces[1][packed(geo, x, j), :] = right


def y_pass(src, pace, geo, emit):
    ny = geo[0]

    def row(x):
        paces = [load_tile(pace, geo, x, j) for j in range(ny)]
        u = [load_tile(src, geo, x, j) for j in range(-3, ny + 3)]
        for j, value in enumerate(y_terms(u, [speed_sign(p) for p in paces])):
            emit(x, j, u[j + 3], paces[j], value)

    over_rows(geo, row)


def x_pass(src, pace, faces, geo, emit):
    ny, x_lo, x_hi, _ = geo
    unroll = (x_hi - x_lo) // TURNS

    def tile(x, j):
        return load_tile(src, geo, x, j)

    def advance(x, j, state):
        d, e, sixth, g, h, pp0, pp1, p2, ql, qr, left = state
        d2 = tile(x + 3, j) - tile(x + 2, j)
        e2 = 0.5 * (d2 - d)
        g2 = e2 - e
        sixth2 = g2 * (1.0 / 6.0)
        pp2, pt2, pm2, half = pair_weights(e, e2, g2)
        ql2, qr2 = central(d, sixth2, half)
        h2 = sixth2 - sixth
        left2, right = face_values(pp0, p2, pm2, h, h2, ql, qr)
        return left, right, (d2, e2, sixth2, g2, h2, pp1, pp2, pt2, ql2, qr2, left2)

    def column(j, carry):
        zero = jnp.zeros((8, NZ), F32)
        x = x_lo - 1
        u = [tile(x + k, j) for k in range(-2, 3)]
        ds = [u[k + 1] - u[k] for k in range(4)]
        es = [0.5 * (ds[k + 1] - ds[k]) for k in range(3)]
        g0, g1 = es[1] - es[0], es[2] - es[1]
        ppa, _, _, _ = pair_weights(es[0], es[1], g0)
        ppb, ptb, _, half = pair_weights(es[1], es[2], g1)
        s0, s1 = g0 * (1.0 / 6.0), g1 * (1.0 / 6.0)
        ql, qr = central(ds[2], s1, half)
        state = (ds[3], es[2], s1, g1, s1 - s0, ppa, ppb, ptb, ql, qr, zero)
        _, _, state = advance(x, j, state)

        def body(i, state):
            for k in range(unroll):
                x = x_lo + i * unroll + k
                left, right, state = advance(x, j, state)
                at = packed(geo, x, j)
                z_left, z_right = prev_z(faces[0][at, :]), faces[1][at, :]
                if pace is None:
                    rising = rise(left, right) + rise(z_left, z_right)
                    falling = fall(left, right) + fall(z_left, z_right)
                    emit(x, j, tile(x, j), rising, falling)
                    continue
                p = load_tile(pace, geo, x, j)
                sign = speed_sign(p)
                total = upwind(sign, left, right) + upwind(sign, z_left, z_right)
                emit(x, j, tile(x, j), p, total)
            return state

        lax.fori_loop(0, TURNS, body, state)
        return carry

    lax.fori_loop(0, ny, column, 0)


def stage(src, slopes, pace, term, faces, geo, finish):
    def keep(x, j, u, p, value):
        term[packed(geo, x, j), :] = value
        z_row(slopes, faces, geo, x, j)

    def join(x, j, u, p, value):
        finish(x, j, u, u + p * root(value + term[packed(geo, x, j), :]))

    y_pass(src, pace, geo, keep)
    x_pass(src, pace, faces, geo, join)


def fill_block(ext, own, before, after, width, slopes=None):
    def put(src, x_to, count, group):
        def body(n, carry):
            for k in range(group):
                x = n * group + k
                for i in range(CY // 8):
                    value = src[pl.ds(pl.multiple_of(x * CY + 8 * i, 8), 8), :]
                    at = pl.ds(pl.multiple_of((x + x_to) * YP + (YO + 8 * i), 8), 8)
                    ext[at, :] = value
                    if slopes:
                        slopes[0][at, :], slopes[1][at, :] = z_slopes(value)
            return carry

        lax.fori_loop(0, count // group, body, 0)

    put(own, XO, CX, 8)
    put(before, XO - width, width, width)
    put(after, XO + CX, width, width)


def fill_sides(ext, before, after, width, slopes=None):
    for t in range(width):
        for b in range(XR // 8):
            for src, y in ((before, YO - width + t), (after, YO + CY + t)):
                value = src[pl.ds(t * XR + 8 * b, 8), :]
                at = pl.ds(b * 8 * YP + y, 8, stride=YP)
                ext[at, :] = value
                if slopes:
                    slopes[0][at, :], slopes[1][at, :] = z_slopes(value)


def sides_kernel(width, own, before, after, low, high, ext):
    fill_block(ext, own, before, after, width)
    for t in range(width):
        for b in range(XR // 8):
            low[pl.ds(t * XR + 8 * b, 8), :] = ext[pl.ds(b * 8 * YP + (YO + t), 8, stride=YP), :]
            high[pl.ds(t * XR + 8 * b, 8), :] = ext[
                pl.ds(b * 8 * YP + (YO + CY - width + t), 8, stride=YP), :
            ]


def params():
    return pltpu.CompilerParams(vmem_limit_bytes=VMEM_LIMIT)


def shape(rows):
    return jax.ShapeDtypeStruct((rows, NZ), F32)


def vmem(rows):
    return pltpu.VMEM((rows, NZ), F32)


def shift_pair(low, high, axis):
    size = lax.axis_size(axis)
    up = [(i, (i + 1) % size) for i in range(size)]
    down = [(j, i) for i, j in up]
    return lax.ppermute(high, axis, up), lax.ppermute(low, axis, down)


def sides_call(pieces, width):
    return pl.pallas_call(
        functools.partial(sides_kernel, width),
        out_shape=(shape(width * XR), shape(width * XR)),
        scratch_shapes=[vmem(EXT)],
        compiler_params=params(),
        cost_estimate=cost(1),
        name="sides",
    )(*pieces)


def cross_x(own, low, high, width):
    pieces = (own, *shift_pair(low, high, "gx"))
    return pieces, sides_call(pieces, width)


def cost(us):
    return pl.CostEstimate(
        flops=1000 * us, bytes_accessed=int(3.0e6 * us), transcendentals=0
    )


def own_geometry(width):
    _, x_lo, x_hi, _ = geometry(width, width - 3)
    return (CY // 8, x_lo, x_hi, YO)


def early_kernel(width, signed, *refs):
    refs = list(refs)
    own, before, after = refs[:3]
    refs = refs[3:]
    pace = refs.pop(0) if signed else None
    outs = [refs.pop(0) for _ in range(1 if signed else 2)]
    base, slopes, faces = refs[0], refs[1:3], refs[3:5]
    fill_block(base, own, before, after, width, slopes)
    geo = own_geometry(width)

    def row(x):
        for j in range(geo[0]):
            z_row(slopes, faces, geo, x, j)

    over_rows(geo, row)

    def emit(x, j, u, *values):
        for out, value in zip(outs, values[-len(outs) :]):
            out[packed(geo, x, j), :] = value

    x_pass(base, pace, faces, geo, emit)


def early_call(width, pieces, pace=None):
    signed = pace is not None
    return pl.pallas_call(
        functools.partial(early_kernel, width, signed),
        out_shape=(shape(XR * CY),) * (1 if signed else 2),
        scratch_shapes=[vmem(EXT)] * 3 + [vmem(XR * CY)] * 2,
        compiler_params=params(),
        cost_estimate=cost(10),
        name="early",
    )(*pieces, *((pace,) if signed else ()))


def runge_kutta(width, next_width, make_pace, *refs):
    refs = list(refs)
    own, before, after, left, right = refs[:5]
    refs = refs[5:]
    early = [refs.pop(0) for _ in range(2 if make_pace else 1)]
    if make_pace:
        p_own, p_before, p_after, p_left, p_right = refs[:5]
        refs = refs[5:]
    else:
        pace = refs.pop(0)
    out = refs.pop(0)
    if next_width:
        out_low, out_high = refs[:2]
        refs = refs[2:]
    if make_pace:
        pace = refs.pop(0)
    base, first, second = refs[:3]
    even, odd, term, faces = refs[3:5], refs[5:7], refs[7], refs[8:10]

    fill_block(base, own, before, after, width)
    fill_sides(base, left, right, width, even)
    if make_pace:
        fill_block(pace, p_own, p_before, p_after, SPEED_HALO)
        fill_sides(pace, p_left, p_right, SPEED_HALO)

    def finish_one(geo):
        def finish(x, j, u, moved):
            store_tile(first, geo, x, j, moved)
            store_slopes(odd, geo, x, j, moved)

        return finish

    inner = own_geometry(width)
    done = finish_one(inner)

    def join(x, j, u, p, value):
        at = packed(inner, x, j)
        if make_pace:
            value += jnp.where(p <= 0.0, early[0][at, :], early[1][at, :])
        else:
            value += early[0][at, :]
        done(x, j, u, u + p * root(value))

    y_pass(base, pace, inner, join)
    for y_lo in (YO - 8, YO + CY):
        side = (1, inner[1], inner[2], y_lo)
        stage(base, even, pace, term, faces, side, finish_one(side))

    geo2 = geometry(width, width - 6)

    def finish_two(x, j, u, moved):
        value = 0.75 * load_tile(base, geo2, x, j) + 0.25 * moved
        store_tile(second, geo2, x, j, value)
        store_slopes(even, geo2, x, j, value)

    stage(first, odd, pace, term, faces, geo2, finish_two)

    geo3 = geometry(width, width - 9)

    def finish_three(x, j, u, moved):
        value = (1.0 / 3.0) * load_tile(base, geo3, x, j) + (2.0 / 3.0) * moved
        if next_width:
            out[pl.ds((x - XO) * CY + j, 8, stride=geo3[0]), :] = value
        else:
            store_tile(first, geo3, x, j, value)

    stage(second, even, pace, term, faces, geo3, finish_three)

    if next_width:
        rows = next_width * CY
        out_low[...] = out[pl.ds(0, rows), :]
        out_high[...] = out[pl.ds(COLS - rows, rows), :]
        return

    def sweep(src, geo, store):
        ny = geo[0]

        def row(x):
            u = [load_tile(src, geo, x, j) for j in range(-1, ny + 1)]
            for j in range(ny):
                v = u[j + 1]
                advected = load_tile(first, geo, x, j)
                sign = sign_of(advected)
                total = upwind(sign, v - u[j], v - u[j + 2])
                total += upwind(
                    sign,
                    v - load_tile(src, geo, x - 1, j),
                    v - load_tile(src, geo, x + 1, j),
                )
                total += upwind(sign, v - prev_z(v), v - next_z(v))
                smooth = advected * lax.rsqrt(advected * advected + 1.0)
                store(x, j, v - PSEUDO_STEP * smooth * (root(total) - 1.0))

        over_rows(geo, row)

    wide, block = geometry(width, 1), geometry(width, 0)
    sweep(first, wide, lambda x, j, v: store_tile(second, wide, x, j, v))

    def store_out(x, j, v):
        out[pl.ds((x - XO) * CY + j, 8, stride=block[0]), :] = v

    sweep(second, block, store_out)


def step_call(width, next_width, pieces, early, pace):
    make_pace = isinstance(pace, tuple)
    outs = [shape(COLS)]
    if next_width:
        outs += [shape(next_width * CY)] * 2
    if make_pace:
        outs += [shape(EXT)]
    return pl.pallas_call(
        functools.partial(runge_kutta, width, next_width, make_pace),
        out_shape=tuple(outs),
        scratch_shapes=[vmem(EXT)] * 7 + [vmem(XR * 56)] * 3,
        compiler_params=params(),
        cost_estimate=cost(35),
        name="step",
    )(*pieces, *early, *(pace if make_pace else (pace,)))


PACK_BLOCK = 2176
UNPACK_BLOCK = 1280


def split(x):
    high = x.astype(jnp.bfloat16)
    low = (x - high.astype(F32)).astype(jnp.bfloat16)
    return jnp.concatenate([high, low], axis=1)


def onehot(mask):
    return jnp.where(mask, 1.0, 0.0).astype(jnp.bfloat16)


def pack_kernel(rows, owner, column, send, parts):
    count = rows.shape[0]
    own = owner[...]
    tags = onehot(lax.broadcasted_iota(jnp.int32, (DEVICES, count), 0) == own)
    order = onehot(
        lax.broadcasted_iota(jnp.int32, (count, count), 0)
        < lax.broadcasted_iota(jnp.int32, (count, count), 1)
    )
    earlier = jnp.dot(tags, order, preferred_element_type=F32)
    rank = jnp.sum(earlier * tags.astype(F32), axis=0, keepdims=True).astype(jnp.int32)
    target = own * SLOTS + rank
    parts[...] = split(rows[...])

    block = PACK_BLOCK

    def body(b, carry):
        slot = lax.broadcasted_iota(jnp.int32, (block, count), 0) + b * block
        both = jnp.dot(onehot(slot == target), parts[...], preferred_element_type=F32)
        send[pl.ds(pl.multiple_of(b * block, block), block), :] = both[:, :NZ] + both[:, NZ:]
        return carry

    lax.fori_loop(0, DEVICES * SLOTS // block, body, 0)

    place = lax.broadcasted_iota(jnp.int32, (NZ, count), 0) == rank
    number = column[...] + 1
    dims = (((1,), (1,)), ((), ()))
    total = jnp.zeros((DEVICES, NZ), F32)
    for part, scale in ((number >> 6, 64.0), (number & 63, 1.0)):
        held = jnp.where(place, part.astype(F32), 0.0).astype(jnp.bfloat16)
        total += scale * lax.dot_general(tags, held, dims, preferred_element_type=F32)
    for b in range(DEVICES // 8):
        send[pl.ds(b * 8 * SLOTS + CAP, 8, stride=SLOTS), :] = total[8 * b : 8 * b + 8]


def unpack_kernel(low_rows, got, mask, speed, speed_low, speed_high, parts, number):
    for b in range(DEVICES // 8):
        number[pl.ds(8 * b, 8), :] = got[pl.ds(b * 8 * SLOTS + CAP, 8, stride=SLOTS), :]
    columns = number[...].T.astype(jnp.int32) - 1
    for k in range(CAP):
        for b in range(DEVICES // 16):
            pair = [
                got[pl.ds((b * 16 + 8 * i) * SLOTS + k, 8, stride=SLOTS), :] for i in range(2)
            ]
            parts[pl.ds(k * DEVICES + 16 * b, 16), :] = split(jnp.concatenate(pair, axis=0))
    named = jnp.concatenate([columns[k : k + 1, :] for k in range(CAP)], axis=1)

    block = UNPACK_BLOCK

    def body(b, carry):
        cell = lax.broadcasted_iota(jnp.int32, (block, CAP * DEVICES), 0) + b * block
        both = jnp.dot(onehot(cell == named), parts[...], preferred_element_type=F32)
        at = pl.ds(pl.multiple_of(b * block, block), block)
        speed[at, :] = (both[:, :NZ] + both[:, NZ:]) * (mask[at, :] * -TIME_STEP)
        return carry

    lax.fori_loop(0, COLS // block, body, 0)
    speed_low[...] = speed[pl.ds(0, low_rows), :]
    speed_high[...] = speed[pl.ds(COLS - low_rows, low_rows), :]


def shards(level_set, band_mask, rows, row_owner, row_tile):
    count = rows.shape[0]
    send = pl.pallas_call(
        pack_kernel,
        out_shape=shape(DEVICES * SLOTS),
        scratch_shapes=[pltpu.VMEM((count, 2 * NZ), jnp.bfloat16)],
        compiler_params=params(),
        cost_estimate=cost(5),
        name="pack",
    )(rows, row_owner.reshape(1, count), row_tile.reshape(1, count))
    u = level_set.reshape(COLS, NZ)
    before, after = shift_pair(u[: 9 * CY], u[COLS - 9 * CY :], "gx")
    send, before, after = lax.optimization_barrier((send, before, after))
    got = lax.all_to_all(
        send.reshape(DEVICES, 1, SLOTS * NZ), ("gx", "gy"), split_axis=0, concat_axis=0, tiled=True
    ).reshape(DEVICES * SLOTS, NZ)
    pieces = (u, before, after)
    sides = sides_call(pieces, 9)
    early = early_call(9, pieces)
    pieces = (*pieces, *shift_pair(*sides, "gy"))
    got, early = lax.optimization_barrier((got, early))

    mask = band_mask.astype(F32).reshape(COLS, 1)
    face = SPEED_HALO * CY
    pace, pace_low, pace_high = pl.pallas_call(
        functools.partial(unpack_kernel, face),
        out_shape=(shape(COLS), shape(face), shape(face)),
        scratch_shapes=[pltpu.VMEM((CAP * DEVICES, 2 * NZ), jnp.bfloat16), vmem(DEVICES)],
        compiler_params=params(),
        name="unpack",
    )(got, mask)
    pace_low, pace_high, pieces = lax.optimization_barrier((pace_low, pace_high, pieces))
    paces, sides = cross_x(pace, pace_low, pace_high, SPEED_HALO)
    paces = (*paces, *shift_pair(*sides, "gy"))
    u, low, high, pace = step_call(9, 9, pieces, early, paces)

    for width, next_width in ((9, 11), (11, 0)):
        pieces, sides = cross_x(u, low, high, width)
        early = early_call(width, pieces, pace)
        pieces = (*pieces, *shift_pair(*sides, "gy"))
        u, *faces = step_call(width, next_width, pieces, early, pace)
        low, high = faces or (None, None)
    return u.reshape(CX, CY, NZ)


def solution(mesh):
    return jax.shard_map(
        shards,
        mesh=mesh,
        in_specs=(
            P("gx", "gy", None),
            P("gx", "gy"),
            P(("gx", "gy"), None),
            P(("gx", "gy"), None),
            P(("gx", "gy")),
        ),
        out_specs=P("gx", "gy", None),
        check_vma=False,
    )
```

```python
import functools

import jax
import jax.numpy as jnp
from jax import lax
from jax.experimental import pallas as pl
from jax.experimental.pallas import tpu as pltpu
from jax.sharding import PartitionSpec as P

EPSILON = 1e-06
TIME_STEP = 0.2
PSEUDO_STEP = 0.3

CX, CY, NZ = 64, 40, 128
DEVICES = 128
CAP = 16
SLOTS = CAP + 1
COLS = CX * CY

XO, YO = 12, 16
XR, YP = 88, 72
EXT = XR * YP
SPEED_HALO = 8
VMEM_LIMIT = 40 * 1024 * 1024
F32 = jnp.float32


def rcp(x):
    return pl.reciprocal(x, approx=True)


QUARTER = 0.25 * EPSILON


def pair_weights(e_left, e_right, g):
    total = e_left + e_right
    half = 0.5 * total
    square = g * g
    centre = half * half + (square * (13.0 / 12.0) + QUARTER)
    ends = centre + square
    cross = total * g
    ip = rcp(ends + cross)
    it = rcp(centre)
    im = rcp(ends - cross)
    return ip * ip, it * it * 3.0, im * im, half


def weight_end(half, g):
    i = rcp(half * half + (g * g * (13.0 / 12.0) + QUARTER))
    return i * i


def central(slope, sixth, half):
    base = slope + sixth
    return base + half, half - base


def face_values(p1, p2, p3, h_left, h_right, q_left, q_right):
    low = p1 * h_left
    high = p3 * h_right
    both = 0.5 * (p1 + p3) + p2
    twice = low + high
    twice = twice + twice
    left = q_left - (twice + high) * rcp(both + p3)
    right = q_right - (twice + low) * rcp(both + p1)
    return left, right


def upwind(sign, left, right):
    top = jnp.maximum(jnp.maximum(sign * left, sign * right), 0.0)
    return top * top


def rise(left, right):
    top = jnp.maximum(jnp.maximum(left, right), 0.0)
    return top * top


def fall(left, right):
    top = jnp.minimum(jnp.minimum(left, right), 0.0)
    return top * top


def sign_of(value):
    return jnp.where(value >= 0.0, 1.0, -1.0)


def speed_sign(pace):
    return jnp.where(pace <= 0.0, 1.0, -1.0)


def root(x):
    return x * lax.rsqrt(jnp.maximum(x, 1e-37))


def prev_z(x):
    return pltpu.roll(x, 1, 1)


def next_z(x):
    return pltpu.roll(x, NZ - 1, 1)


def z_slopes(u):
    after = next_z(u)
    return after - u, 0.5 * (after + prev_z(u)) - u


def z_faces(d, e):
    e_prev, e_next, e_after = prev_z(e), next_z(e), pltpu.roll(e, NZ - 2, 1)
    g_prev, g, g_next = e - e_prev, e_next - e, e_after - e_next
    sixth = g * (1.0 / 6.0)
    h = sixth - g_prev * (1.0 / 6.0)
    h_next = g_next * (1.0 / 6.0) - sixth
    half = 0.5 * (e + e_next)
    pp = weight_end(0.5 * (e_prev + e) + g_prev, g_prev)
    pt = weight_end(half, g) * 3.0
    pm = weight_end(0.5 * (e_next + e_after) - g_next, g_next)
    return face_values(pp, pt, pm, h, h_next, *central(d, sixth, half))


def y_terms(u, signs):
    n = len(u) - 6
    out = []
    d, e, sixth, h, pp, pt, pm, q, left = {}, {}, {}, {}, {}, {}, {}, {}, {}
    d[0] = u[1] - u[0]
    for k in range(1, n + 5):
        d[k] = u[k + 1] - u[k]
        e[k] = 0.5 * (d[k] - d[k - 1])
        if k >= 2:
            f = k - 1
            g = e[k] - e[f]
            sixth[f] = g * (1.0 / 6.0)
            pp[f], pt[f], pm[f], half = pair_weights(e[f], e[k], g)
            q[f] = central(d[f], sixth[f], half)
            if f >= 2:
                h[f] = sixth[f] - sixth[f - 1]
            if f >= 3:
                w = f - 1
                lw, rw = face_values(pp[w - 1], pt[w], pm[w + 1], h[w], h[w + 1], *q[w])
                left[w] = lw
                if w >= 3:
                    out.append(upwind(signs[w - 3], left[w - 1], rw))
    return out


GROUP = 4
ROW_GROUP = 4
SIDE_TURNS = 2
TURNS = 2


def geometry(width, margin):
    count = (CX + 2 * margin + GROUP - 1) // GROUP * GROUP
    return ((CY + 2 * margin + 7) // 8, XO - margin, XO - margin + count, YO - margin)


def load_tile(ref, geo, x, j):
    return ref[pl.ds(x * YP + (geo[3] + j), 8, stride=geo[0]), :]


def store_tile(ref, geo, x, j, value):
    ref[pl.ds(x * YP + (geo[3] + j), 8, stride=geo[0]), :] = value


def store_slopes(slopes, geo, x, j, value):
    d, e = z_slopes(value)
    store_tile(slopes[0], geo, x, j, d)
    store_tile(slopes[1], geo, x, j, e)


def packed(geo, x, j):
    return pl.ds(pl.multiple_of(x * (8 * geo[0]) + 8 * j, 8), 8)


def over_rows(geo, row):
    group = (geo[2] - geo[1]) // SIDE_TURNS if geo[0] == 1 else ROW_GROUP

    def body(i, carry):
        for k in range(group):
            row(geo[1] + i * group + k)
        return carry

    lax.fori_loop(0, (geo[2] - geo[1]) // group, body, 0)


def z_row(slopes, faces, geo, x, j):
    left, right = z_faces(load_tile(slopes[0], geo, x, j), load_tile(slopes[1], geo, x, j))
    faces[0][packed(geo, x, j), :] = left
    faces[1][packed(geo, x, j), :] = right


def y_pass(src, pace, geo, emit):
    ny = geo[0]

    def row(x):
        paces = [load_tile(pace, geo, x, j) for j in range(ny)]
        u = [load_tile(src, geo, x, j) for j in range(-3, ny + 3)]
        for j, value in enumerate(y_terms(u, [speed_sign(p) for p in paces])):
            emit(x, j, u[j + 3], paces[j], value)

    over_rows(geo, row)


def x_pass(src, pace, faces, geo, emit, signs=None):
    ny, x_lo, x_hi, _ = geo
    unroll = (x_hi - x_lo) // TURNS

    def tile(x, j):
        return load_tile(src, geo, x, j)

    def advance(x, j, state):
        d, e, sixth, g, h, pp0, pp1, p2, ql, qr, left = state
        d2 = tile(x + 3, j) - tile(x + 2, j)
        e2 = 0.5 * (d2 - d)
        g2 = e2 - e
        sixth2 = g2 * (1.0 / 6.0)
        pp2, pt2, pm2, half = pair_weights(e, e2, g2)
        ql2, qr2 = central(d, sixth2, half)
        h2 = sixth2 - sixth
        left2, right = face_values(pp0, p2, pm2, h, h2, ql, qr)
        return left, right, (d2, e2, sixth2, g2, h2, pp1, pp2, pt2, ql2, qr2, left2)

    def column(j, carry):
        zero = jnp.zeros((8, NZ), F32)
        x = x_lo - 1
        u = [tile(x + k, j) for k in range(-2, 3)]
        ds = [u[k + 1] - u[k] for k in range(4)]
        es = [0.5 * (ds[k + 1] - ds[k]) for k in range(3)]
        g0, g1 = es[1] - es[0], es[2] - es[1]
        ppa, _, _, _ = pair_weights(es[0], es[1], g0)
        ppb, ptb, _, half = pair_weights(es[1], es[2], g1)
        s0, s1 = g0 * (1.0 / 6.0), g1 * (1.0 / 6.0)
        ql, qr = central(ds[2], s1, half)
        state = (ds[3], es[2], s1, g1, s1 - s0, ppa, ppb, ptb, ql, qr, zero)
        _, _, state = advance(x, j, state)

        def body(i, state):
            for k in range(unroll):
                x = x_lo + i * unroll + k
                left, right, state = advance(x, j, state)
                at = packed(geo, x, j)
                z_left, z_right = prev_z(faces[0][at, :]), faces[1][at, :]
                if pace is None:
                    rising = rise(left, right) + rise(z_left, z_right)
                    falling = fall(left, right) + fall(z_left, z_right)
                    emit(x, j, tile(x, j), rising, falling)
                    continue
                p = load_tile(pace, geo, x, j)
                sign = speed_sign(p) if signs is None else signs[at, :]
                total = upwind(sign, left, right) + upwind(sign, z_left, z_right)
                emit(x, j, tile(x, j), p, total)
            return state

        lax.fori_loop(0, TURNS, body, state)
        return carry

    lax.fori_loop(0, ny, column, 0)


def stage(src, slopes, pace, term, faces, geo, finish):
    signs, *faces = faces

    def keep(x, j, u, p, value):
        term[packed(geo, x, j), :] = value
        signs[packed(geo, x, j), :] = speed_sign(p)
        z_row(slopes, faces, geo, x, j)

    def join(x, j, u, p, value):
        finish(x, j, u, u + p * root(value + term[packed(geo, x, j), :]))

    y_pass(src, pace, geo, keep)
    x_pass(src, pace, faces, geo, join, signs)


def fill_block(ext, own, before, after, width, slopes=None):
    def put(src, x_to, count, group):
        def body(n, carry):
            for k in range(group):
                x = n * group + k
                for i in range(CY // 8):
                    value = src[pl.ds(pl.multiple_of(x * CY + 8 * i, 8), 8), :]
                    at = pl.ds(pl.multiple_of((x + x_to) * YP + (YO + 8 * i), 8), 8)
                    ext[at, :] = value
                    if slopes:
                        slopes[0][at, :], slopes[1][at, :] = z_slopes(value)
            return carry

        lax.fori_loop(0, count // group, body, 0)

    put(own, XO, CX, 8)
    put(before, XO - width, width, width)
    put(after, XO + CX, width, width)


def fill_sides(ext, before, after, width, slopes=None):
    for t in range(width):
        for b in range(XR // 8):
            for src, y in ((before, YO - width + t), (after, YO + CY + t)):
                value = src[pl.ds(t * XR + 8 * b, 8), :]
                at = pl.ds(b * 8 * YP + y, 8, stride=YP)
                ext[at, :] = value
                if slopes:
                    slopes[0][at, :], slopes[1][at, :] = z_slopes(value)


def sides_kernel(width, own, before, after, low, high, ext):
    fill_block(ext, own, before, after, width)
    for t in range(width):
        for b in range(XR // 8):
            low[pl.ds(t * XR + 8 * b, 8), :] = ext[pl.ds(b * 8 * YP + (YO + t), 8, stride=YP), :]
            high[pl.ds(t * XR + 8 * b, 8), :] = ext[
                pl.ds(b * 8 * YP + (YO + CY - width + t), 8, stride=YP), :
            ]


def params():
    return pltpu.CompilerParams(vmem_limit_bytes=VMEM_LIMIT)


def shape(rows):
    return jax.ShapeDtypeStruct((rows, NZ), F32)


def vmem(rows):
    return pltpu.VMEM((rows, NZ), F32)


def shift_pair(low, high, axis):
    size = lax.axis_size(axis)
    up = [(i, (i + 1) % size) for i in range(size)]
    down = [(j, i) for i, j in up]
    return lax.ppermute(high, axis, up), lax.ppermute(low, axis, down)


def sides_call(pieces, width):
    return pl.pallas_call(
        functools.partial(sides_kernel, width),
        out_shape=(shape(width * XR), shape(width * XR)),
        scratch_shapes=[vmem(EXT)],
        compiler_params=params(),
        cost_estimate=cost(1),
        name="sides",
    )(*pieces)


def cross_x(own, low, high, width):
    pieces = (own, *shift_pair(low, high, "gx"))
    return pieces, sides_call(pieces, width)


def cost(us):
    return pl.CostEstimate(
        flops=1000 * us, bytes_accessed=int(3.0e6 * us), transcendentals=0
    )


def own_geometry(width):
    _, x_lo, x_hi, _ = geometry(width, width - 3)
    return (CY // 8, x_lo, x_hi, YO)


def early_kernel(width, signed, *refs):
    refs = list(refs)
    own, before, after = refs[:3]
    refs = refs[3:]
    pace = refs.pop(0) if signed else None
    outs = [refs.pop(0) for _ in range(1 if signed else 2)]
    base, slopes, faces = refs[0], refs[1:3], refs[3:5]
    fill_block(base, own, before, after, width, slopes)
    geo = own_geometry(width)

    def row(x):
        for j in range(geo[0]):
            z_row(slopes, faces, geo, x, j)

    over_rows(geo, row)

    def emit(x, j, u, *values):
        for out, value in zip(outs, values[-len(outs) :]):
            out[packed(geo, x, j), :] = value

    x_pass(base, pace, faces, geo, emit)


def early_call(width, pieces, pace=None):
    signed = pace is not None
    return pl.pallas_call(
        functools.partial(early_kernel, width, signed),
        out_shape=(shape(XR * CY),) * (1 if signed else 2),
        scratch_shapes=[vmem(EXT)] * 3 + [vmem(XR * CY)] * 2,
        compiler_params=params(),
        cost_estimate=cost(10),
        name="early",
    )(*pieces, *((pace,) if signed else ()))


def runge_kutta(width, next_width, make_pace, *refs):
    refs = list(refs)
    own, before, after, left, right = refs[:5]
    refs = refs[5:]
    early = [refs.pop(0) for _ in range(2 if make_pace else 1)]
    if make_pace:
        p_own, p_before, p_after, p_left, p_right = refs[:5]
        refs = refs[5:]
    else:
        pace = refs.pop(0)
    out = refs.pop(0)
    if next_width:
        out_low, out_high = refs[:2]
        refs = refs[2:]
    if make_pace:
        pace = refs.pop(0)
    base, first, second = refs[:3]
    even, odd, term, faces = refs[3:5], refs[5:7], refs[7], refs[8:11]

    fill_block(base, own, before, after, width)
    fill_sides(base, left, right, width, even)
    if make_pace:
        fill_block(pace, p_own, p_before, p_after, SPEED_HALO)
        fill_sides(pace, p_left, p_right, SPEED_HALO)

    def finish_one(geo):
        def finish(x, j, u, moved):
            store_tile(first, geo, x, j, moved)
            store_slopes(odd, geo, x, j, moved)

        return finish

    inner = own_geometry(width)
    done = finish_one(inner)

    def join(x, j, u, p, value):
        at = packed(inner, x, j)
        if make_pace:
            value += jnp.where(p <= 0.0, early[0][at, :], early[1][at, :])
        else:
            value += early[0][at, :]
        done(x, j, u, u + p * root(value))

    y_pass(base, pace, inner, join)
    for y_lo in (YO - 8, YO + CY):
        side = (1, inner[1], inner[2], y_lo)
        stage(base, even, pace, term, faces, side, finish_one(side))

    geo2 = geometry(width, width - 6)

    def finish_two(x, j, u, moved):
        value = 0.75 * load_tile(base, geo2, x, j) + 0.25 * moved
        store_tile(second, geo2, x, j, value)
        store_slopes(even, geo2, x, j, value)

    stage(first, odd, pace, term, faces, geo2, finish_two)

    geo3 = geometry(width, width - 9)

    def finish_three(x, j, u, moved):
        value = (1.0 / 3.0) * load_tile(base, geo3, x, j) + (2.0 / 3.0) * moved
        if next_width:
            out[pl.ds((x - XO) * CY + j, 8, stride=geo3[0]), :] = value
        else:
            store_tile(first, geo3, x, j, value)

    stage(second, even, pace, term, faces, geo3, finish_three)

    if next_width:
        rows = next_width * CY
        out_low[...] = out[pl.ds(0, rows), :]
        out_high[...] = out[pl.ds(COLS - rows, rows), :]
        return

    def sweep(src, geo, store):
        ny = geo[0]

        def row(x):
            u = [load_tile(src, geo, x, j) for j in range(-1, ny + 1)]
            for j in range(ny):
                v = u[j + 1]
                advected = load_tile(first, geo, x, j)
                sign = sign_of(advected)
                total = upwind(sign, v - u[j], v - u[j + 2])
                total += upwind(
                    sign,
                    v - load_tile(src, geo, x - 1, j),
                    v - load_tile(src, geo, x + 1, j),
                )
                total += upwind(sign, v - prev_z(v), v - next_z(v))
                smooth = advected * lax.rsqrt(advected * advected + 1.0)
                store(x, j, v - PSEUDO_STEP * smooth * (root(total) - 1.0))

        over_rows(geo, row)

    wide, block = geometry(width, 1), geometry(width, 0)
    sweep(first, wide, lambda x, j, v: store_tile(second, wide, x, j, v))

    def store_out(x, j, v):
        out[pl.ds((x - XO) * CY + j, 8, stride=block[0]), :] = v

    sweep(second, block, store_out)


def step_call(width, next_width, pieces, early, pace):
    make_pace = isinstance(pace, tuple)
    outs = [shape(COLS)]
    if next_width:
        outs += [shape(next_width * CY)] * 2
    if make_pace:
        outs += [shape(EXT)]
    return pl.pallas_call(
        functools.partial(runge_kutta, width, next_width, make_pace),
        out_shape=tuple(outs),
        scratch_shapes=[vmem(EXT)] * 7 + [vmem(XR * 56)] * 4,
        compiler_params=params(),
        cost_estimate=cost(35),
        name="step",
    )(*pieces, *early, *(pace if make_pace else (pace,)))


PACK_BLOCK = 2176
UNPACK_BLOCK = 1280


def split(x):
    high = x.astype(jnp.bfloat16)
    low = (x - high.astype(F32)).astype(jnp.bfloat16)
    return jnp.concatenate([high, low], axis=1)


def onehot(mask):
    return jnp.where(mask, 1.0, 0.0).astype(jnp.bfloat16)


def pack_kernel(rows, owner, column, send, parts):
    count = rows.shape[0]
    own = owner[...]
    tags = onehot(lax.broadcasted_iota(jnp.int32, (DEVICES, count), 0) == own)
    order = onehot(
        lax.broadcasted_iota(jnp.int32, (count, count), 0)
        < lax.broadcasted_iota(jnp.int32, (count, count), 1)
    )
    earlier = jnp.dot(tags, order, preferred_element_type=F32)
    rank = jnp.sum(earlier * tags.astype(F32), axis=0, keepdims=True).astype(jnp.int32)
    target = own * SLOTS + rank
    parts[...] = split(rows[...])

    block = PACK_BLOCK

    def body(b, carry):
        slot = lax.broadcasted_iota(jnp.int32, (block, count), 0) + b * block
        both = jnp.dot(onehot(slot == target), parts[...], preferred_element_type=F32)
        send[pl.ds(pl.multiple_of(b * block, block), block), :] = both[:, :NZ] + both[:, NZ:]
        return carry

    lax.fori_loop(0, DEVICES * SLOTS // block, body, 0)

    place = lax.broadcasted_iota(jnp.int32, (NZ, count), 0) == rank
    number = column[...] + 1
    dims = (((1,), (1,)), ((), ()))
    total = jnp.zeros((DEVICES, NZ), F32)
    for part, scale in ((number >> 6, 64.0), (number & 63, 1.0)):
        held = jnp.where(place, part.astype(F32), 0.0).astype(jnp.bfloat16)
        total += scale * lax.dot_general(tags, held, dims, preferred_element_type=F32)
    for b in range(DEVICES // 8):
        send[pl.ds(b * 8 * SLOTS + CAP, 8, stride=SLOTS), :] = total[8 * b : 8 * b + 8]


def unpack_kernel(low_rows, got, mask, speed, speed_low, speed_high, parts, number):
    for b in range(DEVICES // 8):
        number[pl.ds(8 * b, 8), :] = got[pl.ds(b * 8 * SLOTS + CAP, 8, stride=SLOTS), :]
    columns = number[...].T.astype(jnp.int32) - 1
    for k in range(CAP):
        for b in range(DEVICES // 16):
            pair = [
                got[pl.ds((b * 16 + 8 * i) * SLOTS + k, 8, stride=SLOTS), :] for i in range(2)
            ]
            parts[pl.ds(k * DEVICES + 16 * b, 16), :] = split(jnp.concatenate(pair, axis=0))
    named = jnp.concatenate([columns[k : k + 1, :] for k in range(CAP)], axis=1)

    block = UNPACK_BLOCK

    def body(b, carry):
        cell = lax.broadcasted_iota(jnp.int32, (block, CAP * DEVICES), 0) + b * block
        both = jnp.dot(onehot(cell == named), parts[...], preferred_element_type=F32)
        at = pl.ds(pl.multiple_of(b * block, block), block)
        speed[at, :] = (both[:, :NZ] + both[:, NZ:]) * (mask[at, :] * -TIME_STEP)
        return carry

    lax.fori_loop(0, COLS // block, body, 0)
    speed_low[...] = speed[pl.ds(0, low_rows), :]
    speed_high[...] = speed[pl.ds(COLS - low_rows, low_rows), :]


def shards(level_set, band_mask, rows, row_owner, row_tile):
    count = rows.shape[0]
    send = pl.pallas_call(
        pack_kernel,
        out_shape=shape(DEVICES * SLOTS),
        scratch_shapes=[pltpu.VMEM((count, 2 * NZ), jnp.bfloat16)],
        compiler_params=params(),
        cost_estimate=cost(5),
        name="pack",
    )(rows, row_owner.reshape(1, count), row_tile.reshape(1, count))
    u = level_set.reshape(COLS, NZ)
    before, after = shift_pair(u[: 9 * CY], u[COLS - 9 * CY :], "gx")
    send, before, after = lax.optimization_barrier((send, before, after))
    got = lax.all_to_all(
        send.reshape(DEVICES, 1, SLOTS * NZ), ("gx", "gy"), split_axis=0, concat_axis=0, tiled=True
    ).reshape(DEVICES * SLOTS, NZ)
    pieces = (u, before, after)
    sides = sides_call(pieces, 9)
    early = early_call(9, pieces)
    pieces = (*pieces, *shift_pair(*sides, "gy"))
    got, early = lax.optimization_barrier((got, early))

    mask = band_mask.astype(F32).reshape(COLS, 1)
    face = SPEED_HALO * CY
    pace, pace_low, pace_high = pl.pallas_call(
        functools.partial(unpack_kernel, face),
        out_shape=(shape(COLS), shape(face), shape(face)),
        scratch_shapes=[pltpu.VMEM((CAP * DEVICES, 2 * NZ), jnp.bfloat16), vmem(DEVICES)],
        compiler_params=params(),
        name="unpack",
    )(got, mask)
    pace_low, pace_high, pieces = lax.optimization_barrier((pace_low, pace_high, pieces))
    paces, sides = cross_x(pace, pace_low, pace_high, SPEED_HALO)
    paces = (*paces, *shift_pair(*sides, "gy"))
    u, low, high, pace = step_call(9, 9, pieces, early, paces)

    for width, next_width in ((9, 11), (11, 0)):
        pieces, sides = cross_x(u, low, high, width)
        early = early_call(width, pieces, pace)
        pieces = (*pieces, *shift_pair(*sides, "gy"))
        u, *faces = step_call(width, next_width, pieces, early, pace)
        low, high = faces or (None, None)
    return u.reshape(CX, CY, NZ)


def solution(mesh):
    return jax.shard_map(
        shards,
        mesh=mesh,
        in_specs=(
            P("gx", "gy", None),
            P("gx", "gy"),
            P(("gx", "gy"), None),
            P(("gx", "gy"), None),
            P(("gx", "gy")),
        ),
        out_specs=P("gx", "gy", None),
        check_vma=False,
    )
```
